128 devices in a mesh: dp: 8 (over z, x_hi), tensor: 16 (over x_lo, y, core).
Axes of the slice: x: 4 (x_hi: 2, x_lo: 2; x = x_hi * 2 + x_lo), y: 4, z: 4, core: 2. Of those that a mesh axis runs over, the one named last changes fastest.
Arguments:
- tokens: bfloat16 [2560, 2048], P('dp', 'tensor'), may hold values from -6 to 6
- cotangent: bfloat16 [2560, 2048], P('dp', 'tensor'), may hold values from -6 to 6
- routes: int32 [2560, 4], P('dp'), may hold values from 0 to 5, all different within a row
- segments: int32 [2560], P('dp'), may hold values from 0 to 2, as said below
- parents: int32 [2560], P('dp'), may hold values from 0 to 1, as said below
- positions: int32 [2560], P('dp'), may hold values from 0 to 319, as said below
- norm_one: bfloat16 [2048], replicated, may hold values from 0.5 to 1.5
- w_query: bfloat16 [2048, 2048], P(None, 'tensor'), may hold values from -0.125 to 0.125
- b_query: bfloat16 [2048], P('tensor'), may hold values from -2 to 2
- w_key: bfloat16 [2048, 2048], P(None, 'tensor'), may hold values from -0.125 to 0.125
- b_key: bfloat16 [2048], P('tensor'), may hold values from -2 to 2
- w_value: bfloat16 [2048, 2048], P(None, 'tensor'), may hold values from -0.125 to 0.125
- b_value: bfloat16 [2048], P('tensor'), may hold values from -2 to 2
- w_out: bfloat16 [2048, 2048], P('tensor'), may hold values from -0.75 to 0.75
- norm_two: bfloat16 [2048], replicated, may hold values from 0.5 to 1.5
- router: bfloat16 [2048, 6], replicated, may hold values from -0.0625 to 0.0625
- expert_gate: bfloat16 [6, 2048, 1408], P(None, None, 'tensor'), may hold values from -0.125 to 0.125
- expert_up: bfloat16 [6, 2048, 1408], P(None, None, 'tensor'), may hold values from -0.125 to 0.125
- expert_down: bfloat16 [6, 1408, 2048], P(None, 'tensor'), may hold values from -1.25 to 1.25
- shared_gate: bfloat16 [2048, 5632], P(None, 'tensor'), may hold values from -0.125 to 0.125
- shared_up: bfloat16 [2048, 5632], P(None, 'tensor'), may hold values from -0.125 to 0.125
- shared_down: bfloat16 [5632, 2048], P('tensor'), may hold values from -0.3125 to 0.3125
- shared_switch: bfloat16 [2048], replicated, may hold values from -0.125 to 0.125
Outputs:
- output: bfloat16 [2560, 2048], P('dp', 'tensor')
- input_grad: float32 [2560, 2048], P('dp', 'tensor')
- grad_norm_one: float32 [2048], replicated
- grad_query: float32 [2048, 2048], P(None, 'tensor')
- grad_query_bias: float32 [2048], P('tensor')
- grad_key: float32 [2048, 2048], P(None, 'tensor')
- grad_key_bias: float32 [2048], P('tensor')
- grad_value: float32 [2048, 2048], P(None, 'tensor')
- grad_value_bias: float32 [2048], P('tensor')
- grad_out_proj: float32 [2048, 2048], P('tensor')
- grad_norm_two: float32 [2048], replicated
- grad_router: float32 [2048, 6], replicated
- grad_expert_gate: float32 [6, 2048, 1408], P(None, None, 'tensor')
- grad_expert_up: float32 [6, 2048, 1408], P(None, None, 'tensor')
- grad_expert_down: float32 [6, 1408, 2048], P(None, 'tensor')
- grad_shared_gate: float32 [2048, 5632], P(None, 'tensor')
- grad_shared_up: float32 [2048, 5632], P(None, 'tensor')
- grad_shared_down: float32 [5632, 2048], P('tensor')
- grad_shared_switch: float32 [2048], replicated
The draws below stay inside these ranges and needn't reach their ends.
Inputs may be any that keep to these rules, and one draw needn't show every extreme that they name: `segments`: each tree's tokens come as segment 0 (its trunk), then segment 1, then segment 2; segment 0 is an ancestor of every segment. `parents`: the segment that a token's segment hangs from: 0 in segments 0 and 1, 0 or 1 in segment 2. `positions`: A token's place on its path from its tree's first token. `routes`: each token names 4 different experts.
All inputs are finite; a program needn't handle non-finite values.
Results may differ from the reference program's by a relative error of at most 0.034.
Values may be sent and summed in bfloat16 or wider, within the bound.
No kernel may reach another device: no remote copies, remote signals or barrier semaphores. Data moves between devices by JAX's collectives and lax.ppermute only.
A program may use at most 192 MiB of HBM per device.

```python
import jax
import jax.numpy as jnp
from jax import lax

D = 2048
HEADS = 16
HDIM = 128
EFF = 1408
SHARED = 5632
EXPERTS = 6
TOPK = 4
TRUNK = 256
BRANCH = 32
TREE = 320
TOKENS = 2560


def tree_layout(key):
    tree_count = TOKENS // TREE
    trunk_shift = jax.random.randint(jax.random.fold_in(key, 11), (tree_count,), 0, TRUNK // 8 + 1)
    chained = jax.random.randint(jax.random.fold_in(key, 12), (tree_count,), 0, 2)
    chained = jnp.where(jnp.arange(tree_count) == 0, 1, chained)
    token_place = jnp.arange(TREE, dtype=jnp.int32)[None, :]
    trunk_len = (TRUNK - 2 * trunk_shift)[:, None]
    branch_len = (BRANCH + trunk_shift)[:, None]
    segment = jnp.where(token_place < trunk_len, 0, jnp.where(token_place < trunk_len + branch_len, 1, 2))
    parent = jnp.where(segment == 2, chained[:, None], 0)
    position = jnp.where((segment == 2) & (chained[:, None] == 0), token_place - branch_len, token_place)
    return (segment.reshape(-1).astype(jnp.int32), parent.reshape(-1).astype(jnp.int32), position.reshape(-1).astype(jnp.int32))


def draw_segments(key, part):
    return tree_layout(key)[0]


def draw_parents(key, part):
    return tree_layout(key)[1]


def draw_positions(key, part):
    return tree_layout(key)[2]


def steps_of(key, dims, cuts, least, high):
    def one(dim, parts):
        steps = jax.random.uniform(jax.random.fold_in(jax.random.fold_in(key, 6), dim), (parts,), jnp.float32, least / len(cuts), high / len(cuts))
        return jnp.repeat(jnp.exp(steps), dims[dim] // parts).reshape((-1,) + (1,) * (len(dims) - dim - 1))

    level = one(*cuts[0])
    for cut in cuts[1:]:
        level = level * one(*cut)
    return level


def choose_distinct(own_key, rows, number_of, top, lift):
    order = jax.random.permutation(jax.random.fold_in(own_key, 1), number_of)
    boost = order
    for power in range(3):
        boost = boost * boost // number_of
    boost = boost * lift // number_of
    chance = jax.random.randint(jax.random.fold_in(own_key, 2), (rows, number_of), 0, 4096) + boost
    fixed_rows = jax.random.permutation(jax.random.fold_in(own_key, 3), rows)[jnp.arange(number_of) % rows]
    chance = jnp.where(jnp.arange(rows)[:, None] == fixed_rows[None, :], 1 << 14, chance)
    priority = chance * number_of + jnp.arange(number_of)
    return lax.top_k(priority.astype(jnp.int32), top)[1].astype(jnp.int32)


def gaussian(own_key, shape, spread, reach, cuts=(), kind=jnp.bfloat16):
    factor_of = steps_of(own_key, shape, cuts, -0.22, 0.18) if cuts else 1.0
    drawn = jax.random.normal(own_key, shape, jnp.float32) * spread * factor_of
    return jnp.minimum(jnp.maximum(drawn, -reach), reach).astype(kind)


def setup_inputs(seed: int = 0) -> dict:
    key_list = jax.random.split(jax.random.key(seed), 24)
    tokens = gaussian(key_list[0], (TOKENS, D), 1.0, 6.0, ((0, 8), (1, 16)))
    cotangent = gaussian(key_list[1], (TOKENS, D), 1.0, 6.0, ((0, 8), (1, 16)))
    routes = choose_distinct(key_list[2], TOKENS, EXPERTS, TOPK, 5461)
    segments = draw_segments(jax.random.fold_in(key_list[23], 71), 0)
    parents = draw_parents(jax.random.fold_in(key_list[23], 71), 0)
    positions = draw_positions(jax.random.fold_in(key_list[23], 71), 0)
    norm_one = jnp.clip(1.0 + 0.1 * jax.random.normal(key_list[6], (D,), jnp.float32), 0.5, 1.5).astype(jnp.bfloat16)
    w_query = gaussian(key_list[7], (D, HEADS * HDIM), D ** -0.5, 0.125, ((1, 16),))
    b_query = gaussian(key_list[8], (HEADS * HDIM,), 0.3, 2.0, ((0, 16),))
    w_key = gaussian(key_list[9], (D, HEADS * HDIM), D ** -0.5, 0.125, ((1, 16),))
    b_key = gaussian(key_list[10], (HEADS * HDIM,), 0.3, 2.0, ((0, 16),))
    w_value = gaussian(key_list[11], (D, HEADS * HDIM), D ** -0.5, 0.125, ((1, 16),))
    b_value = gaussian(key_list[12], (HEADS * HDIM,), 0.3, 2.0, ((0, 16),))
    w_out = gaussian(key_list[13], (HEADS * HDIM, D), (HEADS * HDIM // 32) ** -0.5, 0.75, ((0, 16),))
    norm_two = jnp.clip(1.0 + 0.1 * jax.random.normal(key_list[14], (D,), jnp.float32), 0.5, 1.5).astype(jnp.bfloat16)
    router = gaussian(key_list[15], (D, EXPERTS), (4 * D) ** -0.5, 0.0625)
    expert_gate = gaussian(key_list[16], (EXPERTS, D, EFF), D ** -0.5, 0.125, ((2, 16),))
    expert_up = gaussian(key_list[17], (EXPERTS, D, EFF), D ** -0.5, 0.125, ((2, 16),))
    expert_down = gaussian(key_list[18], (EXPERTS, EFF, D), (max(EFF // 64, 1)) ** -0.5, 1.25, ((1, 16),))
    shared_gate = gaussian(key_list[19], (D, SHARED), D ** -0.5, 0.125, ((1, 16),))
    shared_up = gaussian(key_list[20], (D, SHARED), D ** -0.5, 0.125, ((1, 16),))
    shared_down = gaussian(key_list[21], (SHARED, D), (max(SHARED // 16, 1)) ** -0.5, 0.3125, ((0, 16),))
    shared_switch = gaussian(key_list[22], (D,), D ** -0.5, 0.125)
    return {"tokens": tokens, "cotangent": cotangent, "routes": routes, "segments": segments, "parents": parents, "positions": positions, "norm_one": norm_one, "w_query": w_query, "b_query": b_query, "w_key": w_key, "b_key": b_key, "w_value": w_value, "b_value": b_value, "w_out": w_out, "norm_two": norm_two, "router": router, "expert_gate": expert_gate, "expert_up": expert_up, "expert_down": expert_down, "shared_gate": shared_gate, "shared_up": shared_up, "shared_down": shared_down, "shared_switch": shared_switch}


EPSILON = 1e-06
THETA = 1000000.0
NEG_BIG = -1e+30

@jax.custom_vjp
def low(v):
    return lax.optimization_barrier(v.astype(jnp.bfloat16)).astype(jnp.float32)

@jax.custom_vjp
def low_back(v):
    return v

def low_keep(v):
    return (low(v), None)

def low_pass(kept, grad):
    return (grad,)

def back_keep(v):
    return (v, None)

def back_low(kept, grad):
    return (low(grad),)
low.defvjp(low_keep, low_pass)
low_back.defvjp(back_keep, back_low)

def matmul(left_mat, right_mat):
    return jnp.dot(left_mat, right_mat, precision=lax.Precision.HIGHEST, preferred_element_type=jnp.float32)

def rms_scale(vectors, gain):
    inverse = lax.rsqrt(lax.optimization_barrier(jnp.mean(vectors * vectors, axis=-1, keepdims=True)) + EPSILON)
    return vectors * inverse * gain

def rotary(vectors, cosine, sine_table):
    half_dim = HDIM // 2
    first_half = vectors[..., :half_dim]
    second_half = vectors[..., half_dim:]
    return jnp.concatenate([first_half * cosine - second_half * sine_table, second_half * cosine + first_half * sine_table], axis=-1)

def tree_attention(packed):
    query_rows, key_rows, value_rows, seg_row, parent_row, pos_row = packed
    visible = ((seg_row[None, :] == 0) | (seg_row[None, :] == seg_row[:, None]) | (seg_row[None, :] == parent_row[:, None])) & (pos_row[None, :] <= pos_row[:, None])
    scores = jnp.einsum('qhd,khd->hqk', query_rows, key_rows, precision=lax.Precision.HIGHEST) * HDIM ** (-0.5)
    scores = low_back(scores)
    masked = jnp.where(visible[None], scores, NEG_BIG)
    probs = jax.nn.softmax(masked, axis=-1)
    mixed_heads = jnp.einsum('hqk,khd->qhd', low(probs), value_rows, precision=lax.Precision.HIGHEST)
    return low(low_back(mixed_heads))

def forward(tokens, params, cosine, sine_table, segments, parents, positions, chosen):
    norm_one, w_query, b_query, w_key, b_key, w_value, b_value, w_out, norm_two, router, expert_gate, expert_up, expert_down, shared_gate, shared_up, shared_down, shared_switch = params
    token_count = tokens.shape[0]
    hidden_one = low(rms_scale(tokens, norm_one))
    q_pre = low_back(matmul(hidden_one, w_query) + b_query).reshape(token_count, HEADS, HDIM)
    k_pre = low_back(matmul(hidden_one, w_key) + b_key).reshape(token_count, HEADS, HDIM)
    v_pre = low_back(matmul(hidden_one, w_value) + b_value).reshape(token_count, HEADS, HDIM)
    query_rows = low(rotary(q_pre, cosine, sine_table))
    key_rows = low(rotary(k_pre, cosine, sine_table))
    value_rows = low(v_pre)
    tree_count = token_count // TREE
    packed = (query_rows.reshape(tree_count, TREE, HEADS, HDIM), key_rows.reshape(tree_count, TREE, HEADS, HDIM), value_rows.reshape(tree_count, TREE, HEADS, HDIM), segments.reshape(tree_count, TREE), parents.reshape(tree_count, TREE), positions.reshape(tree_count, TREE))
    mixed = lax.map(jax.checkpoint(tree_attention), packed).reshape(token_count, HEADS * HDIM)
    residual = tokens + low_back(matmul(mixed, w_out))
    hidden_two = low(rms_scale(residual, norm_two))
    logits = low_back(matmul(hidden_two, router))
    mix_weights = jax.nn.softmax(logits, axis=-1) * chosen
    ffn_total = jnp.zeros_like(residual)
    for expert_id in range(EXPERTS):
        gate_val = low_back(matmul(hidden_two, expert_gate[expert_id]))
        up_val = low_back(matmul(hidden_two, expert_up[expert_id]))
        act_val = low(jax.nn.silu(gate_val) * up_val)
        branch_out = low_back(matmul(act_val, expert_down[expert_id]))
        ffn_total = ffn_total + mix_weights[:, expert_id:expert_id + 1] * branch_out
    switch = jax.nn.sigmoid(low_back(matmul(hidden_two, shared_switch[:, None])))
    shared_gate_val = low_back(matmul(hidden_two, shared_gate))
    shared_up_val = low_back(matmul(hidden_two, shared_up))
    shared_act = low(jax.nn.silu(shared_gate_val) * shared_up_val)
    shared_branch = low_back(matmul(shared_act, shared_down))
    return residual + ffn_total + switch * shared_branch

def reference(tokens, cotangent, routes, segments, parents, positions, norm_one, w_query, b_query, w_key, b_key, w_value, b_value, w_out, norm_two, router, expert_gate, expert_up, expert_down, shared_gate, shared_up, shared_down, shared_switch):
    params = tuple((weight.astype(jnp.float32) for weight in (norm_one, w_query, b_query, w_key, b_key, w_value, b_value, w_out, norm_two, router, expert_gate, expert_up, expert_down, shared_gate, shared_up, shared_down, shared_switch)))
    half_dim = HDIM // 2
    frequency = jnp.power(THETA, -2.0 * jnp.arange(half_dim, dtype=jnp.float32) / HDIM)
    angles = positions.astype(jnp.float32)[:, None] * frequency[None, :]
    cosine = jnp.cos(angles)[:, None, :]
    sine_table = jnp.sin(angles)[:, None, :]
    expert_ids = jnp.arange(EXPERTS).astype(jnp.int32)
    chosen = jnp.any(routes[:, :, None] == expert_ids[None, None, :], axis=1).astype(jnp.float32)

    def layer(token_vals, weights):
        return forward(token_vals, weights, cosine, sine_table, segments, parents, positions, chosen)
    output, pullback = jax.vjp(layer, tokens.astype(jnp.float32), params)
    input_grad, param_grads = pullback(cotangent.astype(jnp.float32))
    grad_norm_one, grad_query, grad_query_bias, grad_key, grad_key_bias, grad_value, grad_value_bias, grad_out_proj, grad_norm_two, grad_router, grad_expert_gate, grad_expert_up, grad_expert_down, grad_shared_gate, grad_shared_up, grad_shared_down, grad_shared_switch = param_grads
    return (output.astype(jnp.bfloat16), input_grad, grad_norm_one, grad_query, grad_query_bias, grad_key, grad_key_bias, grad_value, grad_value_bias, grad_out_proj, grad_norm_two, grad_router, grad_expert_gate, grad_expert_up, grad_expert_down, grad_shared_gate, grad_shared_up, grad_shared_down, grad_shared_switch)
```

```python
import jax
import jax.numpy as jnp
from jax import lax
from jax.sharding import Mesh
from jax.sharding import PartitionSpec as P

HDIM = 128
HALF = HDIM // 2
EPSILON = 1e-06
THETA = 1000000.0
NEG_BIG = -1e30
TREES = ("z", "xhi")
TENSOR = ("xlo", "y", "core")
NDP = 8
NTP = 16
ROWS = 320
COLS = 128
WIDTH = 2048
EXPERTS = 6
EFF = 88
ROUTED = EXPERTS * EFF
SHARED = 352
HIDDEN = ROUTED + SHARED
f32 = jnp.float32
bf16 = jnp.bfloat16


def dot_plain(left_mat, right_mat):
    return jnp.dot(left_mat, right_mat, preferred_element_type=f32)


def dot_last(left_mat, right_mat):
    return lax.dot_general(
        left_mat, right_mat, (((1,), (1,)), ((), ())), preferred_element_type=f32
    )


def dot_first(left_mat, right_mat):
    return lax.dot_general(
        left_mat, right_mat, (((0,), (0,)), ((), ())), preferred_element_type=f32
    )


def spread(block, axes, count):
    return lax.all_to_all(
        jnp.broadcast_to(block[None], (count,) + block.shape), axes, 0, 0
    )


def side_by_side(blocks):
    return jnp.transpose(blocks, (1, 0, 2)).reshape(blocks.shape[1], -1)


def cut_columns(rows):
    return jnp.transpose(rows.reshape(rows.shape[0], -1, COLS), (1, 0, 2))


def halves(values):
    high = lax.reduce_precision(values, 8, 7)
    return high.astype(bf16), (values - high).astype(bf16)


def rotate(rows, cosine, sine_table):
    first, second = rows[:, :HALF], rows[:, HALF:]
    return jnp.concatenate(
        [first * cosine - second * sine_table, second * cosine + first * sine_table], axis=1
    )


def per_hidden(weights):
    count = weights.shape[1]
    routed = jnp.broadcast_to(weights[:EXPERTS, None, :], (EXPERTS, EFF, count))
    shared = jnp.broadcast_to(weights[EXPERTS:], (SHARED, count))
    return jnp.concatenate([routed.reshape(ROUTED, count), shared], axis=0)


def per_expert(values):
    count = values.shape[1]
    routed = jnp.sum(values[:ROUTED].reshape(EXPERTS, EFF, count), axis=1)
    return jnp.concatenate([routed, jnp.sum(values[ROUTED:], axis=0, keepdims=True)], axis=0)


def expert_terms(gate_val, up_val, grad_plain, mixing):
    sigma = jax.nn.sigmoid(gate_val)
    silu = gate_val * sigma
    act = silu * up_val
    grad_act = mixing * grad_plain
    grad_gate = grad_act * up_val * sigma * (1.0 + gate_val * (1.0 - sigma))
    grad_up = grad_act * silu
    return act, grad_gate, grad_up


def on_device(
    tokens,
    cotangent,
    routes,
    segments,
    parents,
    positions,
    norm_one,
    w_query,
    b_query,
    w_key,
    b_key,
    w_value,
    b_value,
    w_out,
    norm_two,
    router,
    expert_gate,
    expert_up,
    expert_down,
    shared_gate,
    shared_up,
    shared_down,
    shared_switch,
):
    tree = lax.axis_index(TREES)
    col_start = lax.axis_index(TENSOR) * COLS
    gain_one = norm_one.astype(f32)
    gain_two = norm_two.astype(f32)
    gain_two_cols = lax.dynamic_slice_in_dim(gain_two, col_start, COLS, 0)
    gain_one_cols = lax.dynamic_slice_in_dim(gain_one, col_start, COLS, 0)
    gate_mat = jnp.concatenate(
        [jnp.transpose(expert_gate, (0, 2, 1)).reshape(ROUTED, WIDTH), shared_gate.T], axis=0
    )
    up_mat = jnp.concatenate(
        [jnp.transpose(expert_up, (0, 2, 1)).reshape(ROUTED, WIDTH), shared_up.T], axis=0
    )
    down_mat = jnp.concatenate([expert_down.reshape(ROUTED, WIDTH), shared_down], axis=0)
    w_qkv = jnp.concatenate([w_query, w_key, w_value], axis=1)
    bias = jnp.concatenate([b_query, b_key, b_value]).astype(f32)
    switch_mat = jnp.concatenate([router.T, shared_switch[None]], axis=0)

    cot_blocks = lax.all_gather(cotangent, TREES + TENSOR, axis=0)
    whole_cot = jnp.transpose(
        cot_blocks.reshape(NDP, NTP, ROWS, COLS), (0, 2, 1, 3)
    ).reshape(NDP * ROWS, WIDTH)

    whole_in = side_by_side(spread(tokens, TENSOR, NTP)).astype(f32)
    inverse_one = lax.rsqrt(jnp.mean(whole_in * whole_in, axis=1, keepdims=True) + EPSILON)
    normed_one = whole_in * inverse_one
    hidden_one = (normed_one * gain_one).astype(bf16)
    frequency = jnp.power(THETA, -2.0 * jnp.arange(HALF, dtype=f32) / HDIM)
    angles = positions.astype(f32)[:, None] * frequency[None, :]
    cosine = jnp.cos(angles)
    sine_table = jnp.sin(angles)
    plain = dot_plain(hidden_one, w_qkv)
    biased = plain + bias
    query_rows = rotate(biased[:, :HDIM], cosine, sine_table).astype(bf16)
    key_rows = rotate(biased[:, HDIM : 2 * HDIM], cosine, sine_table).astype(bf16)
    value_rows = biased[:, 2 * HDIM :].astype(bf16)
    visible = (
        (segments[None, :] == 0)
        | (segments[None, :] == segments[:, None])
        | (segments[None, :] == parents[:, None])
    ) & (positions[None, :] <= positions[:, None])
    score_scale = HDIM ** (-0.5)
    scores = dot_last(query_rows, key_rows) * score_scale
    masked = jnp.where(visible, scores, NEG_BIG)
    top_score = jnp.max(masked, axis=1, keepdims=True)
    exp_scores = jnp.exp(masked - top_score)
    row_total = jnp.sum(exp_scores, axis=1, keepdims=True)
    probs = exp_scores / row_total
    probs_low = probs.astype(bf16)
    mixed = dot_plain(probs_low, value_rows).astype(bf16)
    mixer_part = dot_plain(mixed, w_out).astype(bf16)
    mixer_cols = jnp.sum(
        lax.all_to_all(cut_columns(mixer_part), TENSOR, 0, 0).astype(f32), axis=0
    )
    resid_cols = tokens.astype(f32) + mixer_cols
    resid_low = resid_cols.astype(bf16)

    resid_blocks = lax.all_gather(resid_low, TREES + TENSOR, axis=0)
    residual = side_by_side(spread(resid_low, TENSOR, NTP)).astype(f32)
    inverse_two = lax.rsqrt(jnp.mean(residual * residual, axis=1, keepdims=True) + EPSILON)
    hidden_two = (residual * inverse_two * gain_two).astype(bf16)
    logits = dot_last(switch_mat, hidden_two)
    gate_probs = jax.nn.softmax(logits[:EXPERTS], axis=0)
    switch = jax.nn.sigmoid(logits[EXPERTS:])
    expert_ids = jnp.arange(EXPERTS, dtype=jnp.int32)
    chosen = jnp.any(routes.T[None] == expert_ids[:, None, None], axis=1).astype(f32)
    mixing = jnp.concatenate([gate_probs * chosen, switch], axis=0)
    mixing_all = spread(mixing, TREES, NDP)

    grad_plain_all = dot_last(down_mat, whole_cot)
    grad_plain = lax.dynamic_slice_in_dim(grad_plain_all, tree * ROWS, ROWS, 1)
    gate_val = dot_last(gate_mat, hidden_two)
    up_val = dot_last(up_mat, hidden_two)
    spread_mix = per_hidden(mixing)
    act, grad_gate, grad_up = expert_terms(gate_val, up_val, grad_plain, spread_mix)
    mix_part = per_expert(act * grad_plain)
    stat_part = jnp.sum(grad_gate * gate_val + grad_up * up_val, axis=0, keepdims=True)
    high, low = halves(jnp.concatenate([mix_part, stat_part], axis=0))
    extras = jnp.concatenate([high, low], axis=0).reshape(-1, COLS)
    grad_part = dot_first(grad_gate.astype(bf16), gate_mat) + dot_first(
        grad_up.astype(bf16), up_mat
    )
    payload = jnp.concatenate(
        [
            cut_columns(grad_part.astype(bf16)),
            jnp.broadcast_to(extras[None], (NTP,) + extras.shape),
        ],
        axis=1,
    )
    arrived = lax.all_to_all(payload, TENSOR, 0, 0).astype(f32)
    ffn_part = dot_first((spread_mix * act).astype(bf16), down_mat).astype(bf16)
    ffn_cols = jnp.sum(
        lax.all_to_all(cut_columns(ffn_part), TENSOR, 0, 0).astype(f32), axis=0
    )
    output = (resid_cols + ffn_cols).astype(bf16)

    summed = jnp.sum(arrived, axis=0)
    sums = jnp.sum(summed[ROWS:].reshape(2, EXPERTS + 2, ROWS), axis=0)
    masked_grad = sums[:EXPERTS] * chosen
    logit_low = (
        gate_probs * (masked_grad - jnp.sum(gate_probs * masked_grad, axis=0, keepdims=True))
    ).astype(bf16)
    switch_low = (sums[EXPERTS : EXPERTS + 1] * switch * (1.0 - switch)).astype(bf16)
    router_low = jnp.concatenate([logit_low, switch_low], axis=0)
    grad_router = dot_plain(router_low, hidden_two)
    switch_cols = lax.dynamic_slice_in_dim(switch_mat, col_start, COLS, 1)
    grad_two = summed[:ROWS] + dot_first(router_low, switch_cols)
    stat_two = sums[EXPERTS + 1] + jnp.sum(router_low.astype(f32) * logits, axis=0)
    resid_used = resid_low.astype(f32)
    normed_two = resid_used * inverse_two
    grad_gain_two = jnp.sum(grad_two * normed_two, axis=0)
    grad_res = (
        inverse_two * (grad_two * gain_two_cols - normed_two * (stat_two / WIDTH)[:, None])
        + cotangent.astype(f32)
    )
    grad_attn = side_by_side(spread(grad_res.astype(bf16), TENSOR, NTP))

    out_part = dot_first(mixed, grad_attn).astype(bf16)
    early = jnp.concatenate(
        [
            out_part.reshape(NDP, -1, COLS),
            jnp.broadcast_to(
                grad_router.astype(bf16).reshape(1, -1, COLS), (NDP, 7 * NTP, COLS)
            ),
        ],
        axis=1,
    )
    early_sum = jnp.sum(lax.all_to_all(early, TREES, 0, 0).astype(f32), axis=0)
    out_rows = early_sum[: ROWS - 64].astype(bf16)
    router_sum = early_sum[ROWS - 64 :].reshape(7, WIDTH)
    grad_heads = dot_last(grad_attn, w_out).astype(bf16)
    dprobs = dot_last(grad_heads, value_rows)
    dscores = probs * (dprobs - jnp.sum(probs * dprobs, axis=1, keepdims=True))
    dscores_low = dscores.astype(bf16)
    dq_low = rotate(
        dot_plain(dscores_low, key_rows) * score_scale, cosine, -sine_table
    ).astype(bf16)
    dk_low = rotate(
        dot_first(dscores_low, query_rows) * score_scale, cosine, -sine_table
    ).astype(bf16)
    dv_low = dot_first(probs_low, grad_heads).astype(bf16)
    d_low = jnp.concatenate([dq_low, dk_low, dv_low], axis=1)
    d_wide = d_low.astype(f32)
    grad_bias = jnp.sum(d_wide, axis=0)
    part_one = dot_last(d_low, w_qkv)
    stat_one = jnp.sum(d_wide * plain, axis=1)
    gain_part = jnp.sum(part_one * normed_one, axis=0)
    high, low = halves(jnp.concatenate([gain_part, stat_one, jnp.zeros((192,), f32)]))
    high_own, low_own = halves(grad_gain_two)
    extras = jnp.concatenate([high, low, high_own, low_own, jnp.zeros((256,), bf16)])
    extras = extras.reshape(-1, COLS)
    payload = jnp.concatenate(
        [
            cut_columns(part_one.astype(bf16)),
            jnp.broadcast_to(extras[None], (NTP,) + extras.shape),
        ],
        axis=1,
    )
    arrived = lax.all_to_all(payload, TENSOR, 0, 0).astype(f32)
    late = jnp.concatenate(
        [cut_columns((d_wide * inverse_one).astype(bf16)).reshape(-1, COLS), out_rows], axis=0
    )
    late_all = spread(late, TREES, NDP)
    summed = jnp.sum(arrived, axis=0)
    grad_one = summed[:ROWS]
    pair = jnp.sum(summed[ROWS : ROWS + 40].reshape(2, -1), axis=0)
    gain_one_sum = pair[:WIDTH]
    stat_one_sum = pair[WIDTH : WIDTH + ROWS]
    gain_two_sum = (arrived[:, ROWS + 40] + arrived[:, ROWS + 41]).reshape(-1)
    normed_cols = tokens.astype(f32) * inverse_one
    input_grad = (
        inverse_one
        * (grad_one * gain_one_cols - normed_cols * (stat_one_sum / WIDTH)[:, None])
        + grad_res
    )
    small = jnp.concatenate([gain_one_sum, gain_two_sum, grad_bias, jnp.zeros((640,), f32)])
    small = jnp.sum(spread(small.reshape(-1, COLS), TREES, NDP), axis=0).reshape(-1)

    whole_resid = (
        jnp.transpose(resid_blocks.reshape(NDP, NTP, ROWS, COLS), (0, 2, 1, 3))
        .reshape(NDP * ROWS, WIDTH)
        .astype(f32)
    )
    inverse_all = lax.rsqrt(jnp.mean(whole_resid * whole_resid, axis=1, keepdims=True) + EPSILON)
    hidden_all = (whole_resid * inverse_all * gain_two).astype(bf16)
    mix_all = per_hidden(jnp.transpose(mixing_all, (1, 0, 2)).reshape(7, -1))
    gate_all = dot_last(gate_mat, hidden_all)
    up_all = dot_last(up_mat, hidden_all)
    act_all, grad_gate_all, grad_up_all = expert_terms(gate_all, up_all, grad_plain_all, mix_all)
    grad_gate_w = dot_plain(grad_gate_all.astype(bf16), hidden_all)
    grad_up_w = dot_plain(grad_up_all.astype(bf16), hidden_all)
    grad_down_w = dot_plain((mix_all * act_all).astype(bf16), whole_cot)

    token_blocks = lax.all_gather(tokens, TREES + TENSOR, axis=0)
    whole_tokens = jnp.transpose(
        token_blocks.reshape(NDP, NTP, ROWS, COLS), (0, 2, 1, 3)
    ).reshape(NDP * ROWS, WIDTH)
    d_all = jnp.transpose(
        late_all[:, : 3 * ROWS].reshape(NDP, 3, ROWS, COLS), (0, 2, 1, 3)
    ).reshape(NDP * ROWS, 3 * COLS)
    grad_qkv = dot_first(whole_tokens, d_all) * gain_one[:, None]
    grad_out_proj = late_all[:, 3 * ROWS :].reshape(COLS, WIDTH).astype(f32)

    def routed_cols(mat):
        return jnp.transpose(mat[:ROUTED].reshape(EXPERTS, EFF, WIDTH), (0, 2, 1))

    return (
        output,
        input_grad,
        small[:WIDTH],
        grad_qkv[:, :COLS],
        small[2 * WIDTH : 2 * WIDTH + COLS],
        grad_qkv[:, COLS : 2 * COLS],
        small[2 * WIDTH + COLS : 2 * WIDTH + 2 * COLS],
        grad_qkv[:, 2 * COLS :],
        small[2 * WIDTH + 2 * COLS : 2 * WIDTH + 3 * COLS],
        grad_out_proj,
        small[WIDTH : 2 * WIDTH],
        router_sum[:EXPERTS].T,
        routed_cols(grad_gate_w),
        routed_cols(grad_up_w),
        grad_down_w[:ROUTED].reshape(EXPERTS, EFF, WIDTH),
        grad_gate_w[ROUTED:].T,
        grad_up_w[ROUTED:].T,
        grad_down_w[ROUTED:],
        router_sum[EXPERTS],
    )


def solution(mesh):
    fine = Mesh(mesh.devices.reshape(4, 2, 2, 4, 2), TREES + TENSOR)
    both = P(TREES, TENSOR)
    cols = P(None, TENSOR)
    placed = (
        both,
        both,
        P(TREES, None),
        P(TREES),
        P(TREES),
        P(TREES),
        P(),
        cols,
        P(TENSOR),
        cols,
        P(TENSOR),
        cols,
        P(TENSOR),
        P(TENSOR, None),
        P(),
        P(),
        P(None, None, TENSOR),
        P(None, None, TENSOR),
        P(None, TENSOR, None),
        cols,
        cols,
        P(TENSOR, None),
        P(),
    )
    return jax.shard_map(
        on_device,
        mesh=fine,
        in_specs=placed,
        out_specs=(
            both,
            both,
            P(),
            cols,
            P(TENSOR),
            cols,
            P(TENSOR),
            cols,
            P(TENSOR),
            P(TENSOR, None),
            P(),
            P(),
            P(None, None, TENSOR),
            P(None, None, TENSOR),
            P(None, TENSOR, None),
            cols,
            cols,
            P(TENSOR, None),
            P(),
        ),
        check_vma=False,
    )
```

```python
import functools

import jax
import jax.numpy as jnp
from jax import lax
from jax.experimental import pallas as pl
from jax.experimental.pallas import tpu as pltpu
from jax.sharding import Mesh
from jax.sharding import PartitionSpec as P

HDIM = 128
HALF = HDIM // 2
EPSILON = 1e-06
THETA = 1000000.0
NEG_BIG = -1e30
TREES = ("z", "xhi")
CHIPS = ("xlo", "y")
TENSOR = ("xlo", "y", "core")
SWAP = [(0, 1), (1, 0)]
NDP = 8
NCHIP = 8
NTP = 16
ROWS = 320
COLS = 128
WIDTH = 2048
EXPERTS = 6
EFF = 88
ROUTED = EXPERTS * EFF
SHARED = 352
HIDDEN = ROUTED + SHARED
ALL_ROWS = NDP * ROWS
EXTRA = 24
SHOWN = 32
SENT = ROWS + 2 * EXTRA
QKV = 3 * HDIM
OUT_CHUNK = HDIM // NDP
QKV_CHUNK = QKV // NDP
SCALE = HDIM ** (-0.5)
f32 = jnp.float32
bf16 = jnp.bfloat16
MIB = 1024 * 1024


def dot_plain(left_mat, right_mat):
    return jnp.dot(left_mat, right_mat, preferred_element_type=f32)


def dot_last(left_mat, right_mat):
    return lax.dot_general(
        left_mat, right_mat, (((1,), (1,)), ((), ())), preferred_element_type=f32
    )


def dot_first(left_mat, right_mat):
    return lax.dot_general(
        left_mat, right_mat, (((0,), (0,)), ((), ())), preferred_element_type=f32
    )


def sds(shape, dtype):
    return jax.ShapeDtypeStruct(shape, dtype)


def call(body, out_shape, args, *, scratch=(), smem=0, flops=0, moved=0, limit=24):
    specs = [pl.BlockSpec(memory_space=pltpu.SMEM)] * smem
    specs += [pl.BlockSpec(memory_space=pltpu.VMEM)] * (len(args) - smem)
    return pl.pallas_call(
        body,
        in_specs=specs,
        out_specs=[pl.BlockSpec(memory_space=pltpu.VMEM)] * len(out_shape),
        out_shape=out_shape,
        scratch_shapes=list(scratch),
        compiler_params=pltpu.CompilerParams(vmem_limit_bytes=limit * MIB),
        cost_estimate=pl.CostEstimate(flops=flops, bytes_accessed=moved, transcendentals=0),
    )(*args)


def lay_rows(rows_ref, core, own_ref, other_ref):
    for chip in range(NCHIP):
        own = pl.multiple_of((2 * chip + core) * COLS, COLS)
        other = pl.multiple_of((2 * chip + 1 - core) * COLS, COLS)
        rows_ref[:, pl.ds(own, COLS)] = own_ref[chip]
        rows_ref[:, pl.ds(other, COLS)] = other_ref[chip]


def part_chips(core, part, keep_ref, send_ref):
    first = core == 0
    for chip in range(NCHIP):
        even = part[:, 2 * chip * COLS : (2 * chip + 1) * COLS]
        odd = part[:, (2 * chip + 1) * COLS : (2 * chip + 2) * COLS]
        keep_ref[chip] = jnp.where(first, even, odd).astype(keep_ref.dtype)
        send_ref[chip] = jnp.where(first, odd, even).astype(send_ref.dtype)


def rotate(rows, cosine, sine_table):
    first, second = rows[:, :HALF], rows[:, HALF:]
    return jnp.concatenate(
        [first * cosine - second * sine_table, second * cosine + first * sine_table], axis=1
    )


def to_row(column):
    return jnp.transpose(jnp.broadcast_to(column, (column.shape[0], COLS)))[:1]


def to_columns(row):
    return jnp.transpose(jnp.broadcast_to(row, (COLS, row.shape[1])))


def sigmoid(values):
    return 0.5 * jnp.tanh(0.5 * values) + 0.5


def per_hidden(weights):
    count = weights.shape[1]
    parts = [jnp.broadcast_to(weights[e : e + 1], (EFF, count)) for e in range(EXPERTS)]
    parts.append(jnp.broadcast_to(weights[EXPERTS : EXPERTS + 1], (SHARED, count)))
    return jnp.concatenate(parts, axis=0)


def routing(rows, inv_row, switch_mat):
    logits = dot_last(switch_mat, rows) * inv_row
    place = lax.broadcasted_iota(jnp.int32, logits.shape, 0)
    shown = jnp.where(place < EXPERTS, logits, NEG_BIG)
    powers = jnp.exp(shown - jnp.max(shown, axis=0, keepdims=True))
    probs = powers / jnp.sum(powers, axis=0, keepdims=True)
    return logits, jnp.where(place == EXPERTS, sigmoid(logits), probs)


def mean_square_inverse(rows):
    wide = rows.astype(f32)
    return lax.rsqrt(jnp.sum(wide * wide, axis=1, keepdims=True) * (1.0 / WIDTH) + EPSILON)


def attend_body(
    core_ref, own_ref, other_ref, w_ref, bias_ref, cos_ref, sin_ref, see_ref, w_out_ref,
    keep_ref, send_ref, rows_ref, inv_ref, plain_ref, qkv_ref, probs_ref, mixed_ref,
):
    core = core_ref[0]
    lay_rows(rows_ref, core, own_ref, other_ref)
    rows = rows_ref[...]
    inverse = mean_square_inverse(rows)
    inv_ref[...] = jnp.broadcast_to(inverse, (ROWS, COLS))
    plain = dot_plain(rows, w_ref[...]) * inverse
    plain_ref[...] = plain
    biased = plain + bias_ref[...]
    cosine, sine_table = cos_ref[...], sin_ref[...]
    query = rotate(biased[:, :HDIM], cosine, sine_table).astype(bf16)
    keys = rotate(biased[:, HDIM : 2 * HDIM], cosine, sine_table).astype(bf16)
    values = biased[:, 2 * HDIM :].astype(bf16)
    qkv_ref[:, :HDIM] = query
    qkv_ref[:, HDIM : 2 * HDIM] = keys
    qkv_ref[:, 2 * HDIM :] = values
    scores = dot_last(query, keys) * SCALE
    masked = jnp.where(see_ref[...] > 0.5, scores, NEG_BIG)
    powers = jnp.exp(masked - jnp.max(masked, axis=1, keepdims=True))
    probs = powers / jnp.sum(powers, axis=1, keepdims=True)
    probs_ref[...] = probs
    mixed = dot_plain(probs.astype(bf16), values).astype(bf16)
    mixed_ref[...] = mixed
    part_chips(core, dot_plain(mixed, w_out_ref[...]), keep_ref, send_ref)


def residual_body(tokens_ref, arrived_ref, resid_ref, wide_ref):
    total = tokens_ref[...].astype(f32)
    for chip in range(NCHIP):
        total = total + arrived_ref[chip].astype(f32)
    resid_ref[...] = total
    low = total.astype(bf16)
    for chip in range(NCHIP):
        wide_ref[chip] = low


def plain_grad_body(core_ref, own_ref, other_ref, down_ref, out_ref, rows_ref):
    lay_rows(rows_ref, core_ref[0], own_ref, other_ref)
    out_ref[...] = dot_last(down_ref[...], rows_ref[...])


def experts_body(
    core_ref, own_ref, other_ref, chosen_ref, switch_ref, gate_ref, up_ref, plain_ref,
    keep_ref, send_ref, act_ref, extra_ref, rows_ref, inv_ref, inv_row_ref, probs_ref, logits_ref,
):
    core = core_ref[0]
    lay_rows(rows_ref, core, own_ref, other_ref)
    rows = rows_ref[...]
    inverse = mean_square_inverse(rows)
    inv_ref[...] = jnp.broadcast_to(inverse, (ROWS, COLS))
    inv_row = to_row(inverse)
    inv_row_ref[...] = inv_row
    logits, probs = routing(rows, inv_row, switch_ref[...])
    logits_ref[...] = logits
    probs_ref[...] = probs
    mixing = probs * chosen_ref[...]
    gate_val = dot_last(gate_ref[...], rows) * inv_row
    up_val = dot_last(up_ref[...], rows) * inv_row
    spread_mix = per_hidden(mixing)
    sigma = sigmoid(gate_val)
    silu = gate_val * sigma
    act = silu * up_val
    grad_plain = plain_ref[...]
    pair = act * grad_plain
    grad_act = spread_mix * grad_plain
    grad_gate = grad_act * up_val * (sigma + silu * (1.0 - sigma))
    grad_up = grad_act * silu
    sums = [
        jnp.sum(pair[e * EFF : (e + 1) * EFF], axis=0, keepdims=True) for e in range(EXPERTS)
    ]
    sums.append(jnp.sum(pair[ROUTED:], axis=0, keepdims=True))
    sums.append(jnp.sum(grad_gate * gate_val + grad_up * up_val, axis=0, keepdims=True))
    sums = jnp.concatenate(sums, axis=0)
    extra_ref[0] = sums[:, :COLS]
    extra_ref[1] = sums[:, COLS : 2 * COLS]
    extra_ref[2] = jnp.concatenate([sums[:, 2 * COLS :], jnp.zeros((8, HALF), f32)], axis=1)
    part = dot_first(grad_gate.astype(bf16), gate_ref[...])
    part = part + dot_first(grad_up.astype(bf16), up_ref[...])
    part_chips(core, part, keep_ref, send_ref)
    act_ref[...] = (spread_mix * act).astype(bf16)


def branches_body(act_ref, down_ref, out_ref):
    part = dot_first(act_ref[...], down_ref[...]).astype(bf16)
    for block in range(NTP):
        out_ref[block * ROWS : (block + 1) * ROWS] = part[:, block * COLS : (block + 1) * COLS]


def payload_body(keep_ref, came_ref, extra_ref, extra_came_ref, out_ref):
    extra = extra_ref[...] + extra_came_ref[...]
    high = extra.astype(bf16)
    low = (extra - high.astype(f32)).astype(bf16)
    for chip in range(NCHIP):
        out_ref[chip, :ROWS] = (keep_ref[chip] + came_ref[chip].astype(f32)).astype(bf16)
        out_ref[chip, ROWS:] = jnp.concatenate([high, low], axis=0)


def second_norm_body(
    core_ref, arrived_ref, probs_ref, chosen_ref, logits_ref, inv_row_ref, switch_ref, cot_ref,
    resid_ref, inv_ref, gain_ref, wide_ref, grad_ref, router_ref, extra_ref,
):
    dn = arrived_ref[0, :ROWS].astype(f32)
    extra = arrived_ref[0, ROWS:].astype(f32)
    for chip in range(1, NCHIP):
        dn = dn + arrived_ref[chip, :ROWS].astype(f32)
        extra = extra + arrived_ref[chip, ROWS:].astype(f32)
    extra = extra[:EXTRA] + extra[EXTRA:]
    sums = jnp.concatenate([extra[:8], extra[8:16], extra[16:24]], axis=1)[:, :ROWS]
    place = lax.broadcasted_iota(jnp.int32, (8, ROWS), 0)
    probs = probs_ref[...]
    routed = place < EXPERTS
    weighed = jnp.where(routed, probs * (sums * chosen_ref[...]), 0.0)
    total = jnp.sum(weighed, axis=0, keepdims=True)
    low = jnp.where(routed, weighed - probs * total, sums * probs * (1.0 - probs))
    low = jnp.where(place <= EXPERTS, low, 0.0).astype(bf16)
    low_wide = low.astype(f32)
    router_ref[...] = (low_wide * inv_row_ref[...]).astype(bf16)
    dn = dn + dot_first(low, switch_ref[...])
    stat = sums[EXPERTS + 1 :] + jnp.sum(low_wide * logits_ref[...], axis=0, keepdims=True)
    inverse = inv_ref[...]
    normed = resid_ref[...].astype(bf16).astype(f32) * inverse
    own = jnp.sum(dn * normed, axis=0, keepdims=True) / gain_ref[...]
    first = core_ref[0] == 0
    spot = lax.broadcasted_iota(jnp.int32, (8, COLS), 0)
    extra_ref[...] = jnp.where(spot == jnp.where(first, 0, 1), own, 0.0)
    grad = inverse * (dn - normed * (to_columns(stat) * (1.0 / WIDTH)))
    grad = grad + cot_ref[...].astype(f32)
    grad_ref[...] = grad
    low_grad = grad.astype(bf16)
    for chip in range(NCHIP):
        wide_ref[chip] = low_grad


def attend_back_body(
    core_ref, own_ref, other_ref, w_out_ref, qkv_ref, probs_ref, mixed_ref, plain_ref, inv_ref,
    cos_ref, sin_ref, w_ref, rows_ref, router_ref, rows_two_ref, gain_two_ref, gain_own_ref,
    keep_ref, send_ref, extra_ref, trees_ref, tail_ref, grad_rows_ref,
):
    core = core_ref[0]
    lay_rows(grad_rows_ref, core, own_ref, other_ref)
    grad_attn = grad_rows_ref[...]
    query, keys = qkv_ref[:, :HDIM], qkv_ref[:, HDIM : 2 * HDIM]
    values = qkv_ref[:, 2 * HDIM :]
    probs = probs_ref[...]
    heads = dot_last(grad_attn, w_out_ref[...]).astype(bf16)
    dprobs = dot_last(heads, values)
    dscores = probs * (dprobs - jnp.sum(probs * dprobs, axis=1, keepdims=True))
    dscores = dscores.astype(bf16)
    cosine, sine_table = cos_ref[...], -sin_ref[...]
    dq = rotate(dot_plain(dscores, keys) * SCALE, cosine, sine_table)
    dk = rotate(dot_first(dscores, query) * SCALE, cosine, sine_table)
    dv = dot_first(probs.astype(bf16), heads)
    d_low = jnp.concatenate([dq, dk, dv], axis=1).astype(bf16)
    d_wide = d_low.astype(f32)
    part = dot_last(d_low, w_ref[...])
    part_chips(core, part, keep_ref, send_ref)
    inverse = inv_ref[...]
    rows = rows_ref[...]
    normed = rows.astype(f32) * inverse[:, :1]
    gains = jnp.sum(part * normed, axis=0, keepdims=True)
    for block in range(NTP):
        extra_ref[block : block + 1] = gains[:, block * COLS : (block + 1) * COLS]
    stat = to_row(jnp.sum(d_wide * plain_ref[...], axis=1, keepdims=True))
    stat = jnp.concatenate([stat, jnp.zeros((1, HALF), f32)], axis=1)
    for block in range(3):
        extra_ref[NTP + block : NTP + block + 1] = stat[:, block * COLS : (block + 1) * COLS]
    extra_ref[NTP + 3 :] = gain_own_ref[: EXTRA - NTP - 3]
    scaled = (d_wide * jnp.concatenate([inverse] * 3, axis=1)).astype(bf16)
    grad_w = dot_first(scaled, rows).astype(bf16)
    grad_out = dot_first(mixed_ref[...], grad_attn).astype(bf16)
    for tree in range(NDP):
        trees_ref[tree, :QKV_CHUNK] = grad_w[tree * QKV_CHUNK : (tree + 1) * QKV_CHUNK]
        trees_ref[tree, QKV_CHUNK:] = grad_out[tree * OUT_CHUNK : (tree + 1) * OUT_CHUNK]
    bias = jnp.sum(d_wide, axis=0, keepdims=True)
    bias = jnp.concatenate([bias, jnp.zeros((1, WIDTH - QKV), f32)], axis=1)
    router = dot_plain(router_ref[...], rows_two_ref[...]) * gain_two_ref[...]
    place = lax.broadcasted_iota(jnp.int32, (8, WIDTH), 0)
    router = jnp.where(place == EXPERTS + 1, bias, router)
    tail_ref[...] = router


def first_norm_body(arrived_ref, tokens_ref, inv_ref, grad_res_ref, out_ref, small_ref):
    dn = arrived_ref[0, :ROWS].astype(f32)
    tails = [arrived_ref[chip, ROWS:].astype(f32) for chip in range(NCHIP)]
    for chip in range(1, NCHIP):
        dn = dn + arrived_ref[chip, :ROWS].astype(f32)
    tails = [tail[:EXTRA] + tail[EXTRA:] for tail in tails]
    extra = sum(tails[1:], tails[0])
    stat = jnp.concatenate([extra[NTP + k : NTP + k + 1] for k in range(3)], axis=1)
    stat = to_columns(stat)[:ROWS] * (1.0 / WIDTH)
    inverse = inv_ref[...]
    normed = tokens_ref[...].astype(f32) * inverse
    out_ref[...] = inverse * (dn - normed * stat) + grad_res_ref[...]
    small_ref[...] = jnp.zeros((8, WIDTH), f32)
    for block in range(NTP):
        spot = slice(block * COLS, (block + 1) * COLS)
        small_ref[0:1, spot] = extra[block : block + 1]
        place = NTP + 3 + block % 2
        small_ref[1:2, spot] = tails[block // 2][place : place + 1]


def trees_body(arrived_ref, tail_ref, small_ref, out_ref):
    total = arrived_ref[0].astype(f32)
    for tree in range(1, NDP):
        total = total + arrived_ref[tree].astype(f32)
    low = total.astype(bf16)
    tail = jnp.concatenate([tail_ref[...], small_ref[...]], axis=0).astype(bf16)
    for tree in range(NDP):
        out_ref[tree, : QKV_CHUNK + OUT_CHUNK] = low
        out_ref[tree, QKV_CHUNK + OUT_CHUNK :] = tail


def last_body(all_ref, gain_ref, query_ref, key_ref, value_ref, out_ref, tail_ref):
    mats = jnp.concatenate([all_ref[tree, :QKV_CHUNK] for tree in range(NDP)], axis=0)
    mats = mats.astype(f32) * gain_ref[...]
    query_ref[...] = jnp.transpose(mats[:HDIM])
    key_ref[...] = jnp.transpose(mats[HDIM : 2 * HDIM])
    value_ref[...] = jnp.transpose(mats[2 * HDIM :])
    start = QKV_CHUNK + OUT_CHUNK
    tail = jnp.zeros((16, WIDTH), f32)
    for tree in range(NDP):
        out_ref[tree * OUT_CHUNK : (tree + 1) * OUT_CHUNK] = all_ref[
            tree, QKV_CHUNK:start
        ].astype(f32)
        tail = tail + all_ref[tree, start:].astype(f32)
    tail_ref[...] = tail


def lay_trees(rows_ref, blocks_ref, trees):
    for tree in range(trees):
        for block in range(NTP):
            rows_ref[tree * ROWS : (tree + 1) * ROWS, block * COLS : (block + 1) * COLS] = (
                blocks_ref[tree, block, :ROWS]
            )


def plain_all_body(blocks_ref, down_ref, out_ref, rows_ref):
    lay_trees(rows_ref, blocks_ref, 2)
    out_ref[...] = dot_last(down_ref[...], rows_ref[...])


def hidden_all_body(
    blocks_ref, plain_ref, chosen_ref, switch_ref, gate_ref, up_ref,
    grad_gate_ref, grad_up_ref, act_ref, rows_ref,
):
    lay_trees(rows_ref, blocks_ref, 2)
    rows = rows_ref[...]
    inverse = to_row(mean_square_inverse(rows))
    chosen = []
    for tree in range(2):
        shown = chosen_ref[tree].astype(f32)
        chosen.append(
            jnp.concatenate([shown[:8], shown[8:16], shown[16:24]], axis=1)[:, :ROWS]
        )
    _, probs = routing(rows, inverse, switch_ref[...])
    mix = probs * jnp.concatenate(chosen, axis=1)
    gate_val = dot_last(gate_ref[...], rows) * inverse
    up_val = dot_last(up_ref[...], rows) * inverse
    spread_mix = per_hidden(mix)
    sigma = sigmoid(gate_val)
    silu = gate_val * sigma
    act_ref[...] = (spread_mix * (silu * up_val)).astype(bf16)
    grad_act = (spread_mix * inverse) * plain_ref[...]
    grad_gate_ref[...] = (grad_act * up_val * (sigma + silu * (1.0 - sigma))).astype(bf16)
    grad_up_ref[...] = (grad_act * silu).astype(bf16)


def weights_body(
    grad_gate_ref, grad_up_ref, act_ref, resid_ref, cot_ref, gain_ref,
    gate_r_ref, gate_s_ref, up_r_ref, up_s_ref, down_r_ref, down_s_ref,
):
    resid = jnp.concatenate(
        [resid_ref[:, k].reshape(ALL_ROWS, COLS) for k in range(2)], axis=1
    )
    cot = jnp.concatenate(
        [cot_ref[:, k, :ROWS].reshape(ALL_ROWS, COLS) for k in range(2)], axis=1
    )
    gain = gain_ref[...]
    grad = dot_plain(grad_gate_ref[...], resid) * gain
    gate_r_ref[...] = grad[:ROUTED]
    gate_s_ref[...] = grad[ROUTED:]
    grad = dot_plain(grad_up_ref[...], resid) * gain
    up_r_ref[...] = grad[:ROUTED]
    up_s_ref[...] = grad[ROUTED:]
    grad = dot_plain(act_ref[...], cot)
    down_r_ref[...] = grad[:ROUTED]
    down_s_ref[...] = grad[ROUTED:]


def once(shape):
    zero = (0,) * len(shape)
    return pl.BlockSpec(shape, lambda i: zero, pipeline_mode=pl.Buffered(1))


PAIR = 2 * ROWS
PAIR_FLOPS = 2 * HIDDEN * WIDTH * ALL_ROWS


def plain_all(blocks, down_mat):
    return pl.pallas_call(
        plain_all_body,
        grid=(NDP // 2,),
        in_specs=[
            pl.BlockSpec((2, NTP, ROWS + SHOWN, COLS), lambda i: (i, 0, 0, 0)),
            once((HIDDEN, WIDTH)),
        ],
        out_specs=pl.BlockSpec((HIDDEN, PAIR), lambda i: (0, i)),
        out_shape=sds((HIDDEN, ALL_ROWS), f32),
        scratch_shapes=[pltpu.VMEM((PAIR, WIDTH), bf16)],
        compiler_params=pltpu.CompilerParams(vmem_limit_bytes=28 * MIB),
        cost_estimate=pl.CostEstimate(
            flops=PAIR_FLOPS, bytes_accessed=23 * MIB, transcendentals=0
        ),
    )(blocks, down_mat)


def hidden_all(blocks, plain, chosen, switch_mat, gate_mat, up_mat):
    return pl.pallas_call(
        hidden_all_body,
        grid=(NDP // 2,),
        in_specs=[
            pl.BlockSpec((2, NTP, ROWS, COLS), lambda i: (i, 0, 0, 0)),
            pl.BlockSpec((HIDDEN, PAIR), lambda i: (0, i)),
            pl.BlockSpec((2, SHOWN, COLS), lambda i: (i, 0, 0)),
            once((8, WIDTH)),
            once((HIDDEN, WIDTH)),
            once((HIDDEN, WIDTH)),
        ],
        out_specs=[pl.BlockSpec((HIDDEN, PAIR), lambda i: (0, i))] * 3,
        out_shape=[sds((HIDDEN, ALL_ROWS), bf16)] * 3,
        scratch_shapes=[pltpu.VMEM((PAIR, WIDTH), bf16)],
        compiler_params=pltpu.CompilerParams(vmem_limit_bytes=44 * MIB),
        cost_estimate=pl.CostEstimate(
            flops=2 * PAIR_FLOPS, bytes_accessed=40 * MIB, transcendentals=HIDDEN * ALL_ROWS
        ),
    )(blocks, plain, chosen, switch_mat, gate_mat, up_mat)


def weight_grads(grad_gate, grad_up, act, resid, cot, gain):
    step = 2 * COLS
    wide = pl.BlockSpec((NDP, 2, ROWS, COLS), lambda i: (0, i, 0, 0))
    tall = pl.BlockSpec((NDP, 2, ROWS + SHOWN, COLS), lambda i: (0, i, 0, 0))
    return pl.pallas_call(
        weights_body,
        grid=(WIDTH // step,),
        in_specs=[
            once((HIDDEN, ALL_ROWS)),
            once((HIDDEN, ALL_ROWS)),
            once((HIDDEN, ALL_ROWS)),
            wide,
            tall,
            pl.BlockSpec((1, step), lambda i: (0, i)),
        ],
        out_specs=[
            pl.BlockSpec((ROUTED, step), lambda i: (0, i)),
            pl.BlockSpec((SHARED, step), lambda i: (0, i)),
        ]
        * 3,
        out_shape=[sds((ROUTED, WIDTH), f32), sds((SHARED, WIDTH), f32)] * 3,
        compiler_params=pltpu.CompilerParams(vmem_limit_bytes=44 * MIB),
        cost_estimate=pl.CostEstimate(
            flops=3 * PAIR_FLOPS, bytes_accessed=56 * MIB, transcendentals=0
        ),
    )(grad_gate, grad_up, act, resid, cot, gain)


def widen(block, count):
    return jnp.broadcast_to(block[None], (count,) + block.shape)


def over_chips(blocks):
    return lax.all_to_all(blocks, CHIPS, 0, 0)


def over_trees(blocks):
    return lax.all_to_all(blocks, TREES, 0, 0)


def after(value, *others):
    return lax.optimization_barrier((value,) + others)[0]


def swap(block):
    return lax.ppermute(block, "core", SWAP)


def on_device(
    tokens,
    cotangent,
    routes,
    segments,
    parents,
    positions,
    norm_one,
    w_query,
    b_query,
    w_key,
    b_key,
    w_value,
    b_value,
    w_out,
    norm_two,
    router,
    expert_gate,
    expert_up,
    expert_down,
    shared_gate,
    shared_up,
    shared_down,
    shared_switch,
):
    core = lax.axis_index("core").astype(jnp.int32).reshape(1)
    col_start = lax.axis_index(TENSOR) * COLS
    gain_one = norm_one.astype(f32)
    gain_two = norm_two.astype(f32)

    def to_hidden(routed, shared):
        mat = jnp.concatenate(
            [jnp.transpose(routed, (0, 2, 1)).reshape(ROUTED, WIDTH), shared.T], axis=0
        )
        return (mat.astype(f32) * gain_two).astype(bf16)

    gate_mat = to_hidden(expert_gate, shared_gate)
    up_mat = to_hidden(expert_up, shared_up)
    down_mat = jnp.concatenate([expert_down.reshape(ROUTED, WIDTH), shared_down], axis=0)
    w_qkv = jnp.concatenate([w_query, w_key, w_value], axis=1)
    w_qkv = (w_qkv.astype(f32) * gain_one[:, None]).astype(bf16)
    bias = jnp.concatenate([b_query, b_key, b_value]).astype(f32)[None]
    switch_mat = jnp.concatenate(
        [router.T, shared_switch[None], jnp.zeros((1, WIDTH), bf16)], axis=0
    )
    switch_mat = (switch_mat.astype(f32) * gain_two).astype(bf16)
    switch_cols = lax.dynamic_slice_in_dim(switch_mat, col_start, COLS, 1)
    gain_two_cols = lax.dynamic_slice_in_dim(gain_two, col_start, COLS, 0)[None]
    frequency = jnp.power(THETA, -2.0 * jnp.arange(HALF, dtype=f32) / HDIM)
    angles = positions.astype(f32)[:, None] * frequency[None, :]
    cosine = jnp.cos(angles)
    sine_table = jnp.sin(angles)
    visible = (
        (segments[None, :] == 0)
        | (segments[None, :] == segments[:, None])
        | (segments[None, :] == parents[:, None])
    ) & (positions[None, :] <= positions[:, None])
    visible = visible.astype(f32)
    expert_ids = jnp.arange(8, dtype=jnp.int32)
    chosen = jnp.any(routes.T[None] == expert_ids[:, None, None], axis=1)
    chosen = (chosen | (expert_ids[:, None] >= EXPERTS)).astype(f32)

    own = over_chips(widen(tokens, NCHIP))
    shown = jnp.pad(chosen, ((0, 0), (0, 2 * HALF - ROWS % COLS)))
    shown = jnp.transpose(shown.reshape(8, 3, COLS), (1, 0, 2)).reshape(EXTRA, COLS)
    shown = jnp.pad(shown, ((0, SHOWN - EXTRA), (0, 0))).astype(bf16)
    cot_blocks = lax.all_gather(
        jnp.concatenate([cotangent, shown], axis=0), TREES + TENSOR, axis=0
    )
    cot_blocks = cot_blocks.reshape(NDP, NTP, ROWS + SHOWN, COLS)
    chosen_all = cot_blocks[:, 0, ROWS:]
    own_cot = over_chips(widen(cotangent, NCHIP))
    other = swap(own)
    blocks8 = (NCHIP, ROWS, COLS)
    keep, send, rows_one, inv_one, plain, qkv, probs, mixed = call(
        attend_body,
        [
            sds(blocks8, f32), sds(blocks8, bf16), sds((ROWS, WIDTH), bf16),
            sds((ROWS, COLS), f32), sds((ROWS, QKV), f32), sds((ROWS, QKV), bf16),
            sds((ROWS, ROWS), f32), sds((ROWS, HDIM), bf16),
        ],
        [core, own, other, w_qkv, bias, cosine, sine_table, visible, w_out],
        smem=1, flops=900_000_000, moved=8 * MIB,
    )
    arrived = over_chips((keep + swap(send).astype(f32)).astype(bf16))
    grad_plain = call(
        plain_grad_body,
        [sds((HIDDEN, ROWS), f32)],
        [core, own_cot, swap(own_cot), down_mat],
        scratch=[pltpu.VMEM((ROWS, WIDTH), bf16)],
        smem=1, flops=2 * HIDDEN * WIDTH * ROWS, moved=6 * MIB,
    )[0]
    resid_cols, wide = call(
        residual_body,
        [sds((ROWS, COLS), f32), sds(blocks8, bf16)],
        [tokens, after(arrived, grad_plain, gate_mat, up_mat)],
        moved=2 * MIB,
    )

    own = over_chips(wide)
    resid_blocks = lax.all_gather(wide[0], TREES + TENSOR, axis=0)
    resid_blocks = resid_blocks.reshape(NDP, NTP, ROWS, COLS)
    (
        keep, send, act, extra, rows_two, inv_two, inv_row, gates, logits,
    ) = call(
        experts_body,
        [
            sds(blocks8, f32), sds(blocks8, bf16), sds((HIDDEN, ROWS), bf16),
            sds((3, 8, COLS), f32), sds((ROWS, WIDTH), bf16), sds((ROWS, COLS), f32),
            sds((1, ROWS), f32), sds((8, ROWS), f32), sds((8, ROWS), f32),
        ],
        [core, own, swap(own), chosen, switch_mat, gate_mat, up_mat, grad_plain],
        smem=1, flops=8 * HIDDEN * WIDTH * ROWS, moved=20 * MIB,
    )
    extra = extra.reshape(EXTRA, COLS)
    payload = call(
        payload_body,
        [sds((NCHIP, SENT, COLS), bf16)],
        [keep, swap(send), extra, swap(extra)],
        moved=4 * MIB,
    )[0]
    arrived = over_chips(payload)
    plain_rows = plain_all(cot_blocks, down_mat)
    wide, grad_res, router_low, gain_own = call(
        second_norm_body,
        [
            sds(blocks8, bf16), sds((ROWS, COLS), f32), sds((8, ROWS), bf16),
            sds((8, COLS), f32),
        ],
        [
            core, after(arrived, plain_rows), gates, chosen, logits, inv_row, switch_cols, cotangent,
            resid_cols,
            inv_two, gain_two_cols,
        ],
        smem=1, moved=3 * MIB,
    )
    own = over_chips(wide)
    ffn = call(
        branches_body,
        [sds((NTP * ROWS, COLS), bf16)],
        [after(act, grad_res), down_mat],
        flops=2 * HIDDEN * WIDTH * ROWS, moved=8 * MIB,
    )[0]
    keep, send, extra, trees, tail = call(
        attend_back_body,
        [
            sds(blocks8, f32), sds(blocks8, bf16), sds((EXTRA, COLS), f32),
            sds((NDP, QKV_CHUNK + OUT_CHUNK, WIDTH), bf16), sds((8, WIDTH), f32),
        ],
        [
            core, own, swap(own), w_out, qkv, probs, mixed, plain, inv_one, cosine, sine_table,
            w_qkv, rows_one, router_low, rows_two, gain_two[None], gain_own,
        ],
        scratch=[pltpu.VMEM((ROWS, WIDTH), bf16)],
        smem=1, flops=2_000_000_000, moved=14 * MIB,
    )
    payload = call(
        payload_body,
        [sds((NCHIP, SENT, COLS), bf16)],
        [keep, swap(send), extra, swap(extra)],
        moved=4 * MIB,
    )[0]
    arrived = over_chips(payload)
    tree_sums = over_trees(trees)
    grads = hidden_all(
        after(resid_blocks, payload), plain_rows, chosen_all, switch_mat, gate_mat, up_mat
    )
    ffn = lax.psum_scatter(
        after(ffn, resid_blocks, payload), TENSOR, scatter_dimension=0, tiled=True
    )
    input_grad, small = call(
        first_norm_body,
        [sds((ROWS, COLS), f32), sds((8, WIDTH), f32)],
        [arrived, tokens, inv_one, grad_res],
        moved=2 * MIB,
    )
    chunk = QKV_CHUNK + OUT_CHUNK
    wide = call(
        trees_body,
        [sds((NDP, chunk + 16, WIDTH), bf16)],
        [after(tree_sums, *grads), tail, small],
        moved=6 * MIB,
    )[0]
    everything = over_trees(wide)
    output = (resid_cols + after(ffn, everything).astype(f32)).astype(bf16)
    grad_query, grad_key, grad_value, grad_out_proj, tail = call(
        last_body,
        [
            sds((WIDTH, HDIM), f32), sds((WIDTH, HDIM), f32), sds((WIDTH, HDIM), f32),
            sds((HDIM, WIDTH), f32), sds((16, WIDTH), f32),
        ],
        [everything, gain_one[None]],
        moved=7 * MIB,
    )

    gate_r, gate_s, up_r, up_s, down_r, down_s = weight_grads(
        after(grads[0], wide, input_grad), *grads[1:], resid_blocks, cot_blocks, gain_two[None]
    )

    def routed_cols(mat):
        return jnp.transpose(mat.reshape(EXPERTS, EFF, WIDTH), (0, 2, 1))

    return (
        output,
        input_grad,
        tail[8] / gain_one,
        grad_query,
        tail[EXPERTS + 1, :HDIM],
        grad_key,
        tail[EXPERTS + 1, HDIM : 2 * HDIM],
        grad_value,
        tail[EXPERTS + 1, 2 * HDIM : QKV],
        grad_out_proj,
        tail[9],
        tail[:EXPERTS].T,
        routed_cols(gate_r),
        routed_cols(up_r),
        down_r.reshape(EXPERTS, EFF, WIDTH),
        gate_s.T,
        up_s.T,
        down_s,
        tail[EXPERTS],
    )


def solution(mesh):
    fine = Mesh(mesh.devices.reshape(4, 2, 2, 4, 2), TREES + TENSOR)
    both = P(TREES, TENSOR)
    cols = P(None, TENSOR)
    placed = (
        both,
        both,
        P(TREES, None),
        P(TREES),
        P(TREES),
        P(TREES),
        P(),
        cols,
        P(TENSOR),
        cols,
        P(TENSOR),
        cols,
        P(TENSOR),
        P(TENSOR, None),
        P(),
        P(),
        P(None, None, TENSOR),
        P(None, None, TENSOR),
        P(None, TENSOR, None),
        cols,
        cols,
        P(TENSOR, None),
        P(),
    )
    return jax.shard_map(
        on_device,
        mesh=fine,
        in_specs=placed,
        out_specs=(
            both,
            both,
            P(),
            cols,
            P(TENSOR),
            cols,
            P(TENSOR),
            cols,
            P(TENSOR),
            P(TENSOR, None),
            P(),
            P(),
            P(None, None, TENSOR),
            P(None, None, TENSOR),
            P(None, TENSOR, None),
            cols,
            cols,
            P(TENSOR, None),
            P(),
        ),
        check_vma=False,
    )
```

```python
import functools

import jax
import jax.numpy as jnp
from jax import lax
from jax.experimental import pallas as pl
from jax.experimental.pallas import tpu as pltpu
from jax.sharding import Mesh
from jax.sharding import PartitionSpec as P

HDIM = 128
HALF = HDIM // 2
EPSILON = 1e-06
THETA = 1000000.0
NEG_BIG = -1e30
TREES = ("z", "xhi")
CHIPS = ("xlo", "y")
TENSOR = ("xlo", "y", "core")
SWAP = [(0, 1), (1, 0)]
NDP = 8
NCHIP = 8
NTP = 16
ROWS = 320
COLS = 128
WIDTH = 2048
EXPERTS = 6
EFF = 88
ROUTED = EXPERTS * EFF
SHARED = 352
HIDDEN = ROUTED + SHARED
ALL_ROWS = NDP * ROWS
EXTRA = 24
SHOWN = 32
SENT = ROWS + 2 * EXTRA
QKV = 3 * HDIM
OUT_CHUNK = HDIM // NDP
QKV_CHUNK = QKV // NDP
SCALE = HDIM ** (-0.5)
f32 = jnp.float32
bf16 = jnp.bfloat16
MIB = 1024 * 1024


def dot_plain(left_mat, right_mat):
    return jnp.dot(left_mat, right_mat, preferred_element_type=f32)


def dot_last(left_mat, right_mat):
    return lax.dot_general(
        left_mat, right_mat, (((1,), (1,)), ((), ())), preferred_element_type=f32
    )


def dot_first(left_mat, right_mat):
    return lax.dot_general(
        left_mat, right_mat, (((0,), (0,)), ((), ())), preferred_element_type=f32
    )


def sds(shape, dtype):
    return jax.ShapeDtypeStruct(shape, dtype)


def call(body, out_shape, args, *, smem=0, flops=0, moved=0, limit=60):
    specs = [pl.BlockSpec(memory_space=pltpu.SMEM)] * smem
    specs += [pl.BlockSpec(memory_space=pltpu.VMEM)] * (len(args) - smem)
    return pl.pallas_call(
        body,
        in_specs=specs,
        out_specs=[pl.BlockSpec(memory_space=pltpu.VMEM)] * len(out_shape),
        out_shape=out_shape,
        compiler_params=pltpu.CompilerParams(vmem_limit_bytes=limit * MIB),
        cost_estimate=pl.CostEstimate(flops=flops, bytes_accessed=moved, transcendentals=0),
    )(*args)


def lay_rows(rows_ref, core, own_ref, other_ref, window=slice(0, ROWS)):
    for chip in range(NCHIP):
        own = pl.multiple_of((2 * chip + core) * COLS, COLS)
        other = pl.multiple_of((2 * chip + 1 - core) * COLS, COLS)
        rows_ref[:, pl.ds(own, COLS)] = own_ref[chip, window]
        rows_ref[:, pl.ds(other, COLS)] = other_ref[chip, window]


def part_chips(core, part, keep_ref, send_ref):
    first = core == 0
    for chip in range(NCHIP):
        even = part[:, 2 * chip * COLS : (2 * chip + 1) * COLS]
        odd = part[:, (2 * chip + 1) * COLS : (2 * chip + 2) * COLS]
        keep_ref[chip] = jnp.where(first, even, odd).astype(keep_ref.dtype)
        send_ref[chip] = jnp.where(first, odd, even).astype(send_ref.dtype)


def rotate(rows, cosine, sine_table):
    first, second = rows[:, :HALF], rows[:, HALF:]
    return jnp.concatenate(
        [first * cosine - second * sine_table, second * cosine + first * sine_table], axis=1
    )


def to_row(column):
    return jnp.transpose(jnp.broadcast_to(column, (column.shape[0], COLS)))[:1]


def to_columns(row):
    return jnp.transpose(jnp.broadcast_to(row, (COLS, row.shape[1])))


def sigmoid(values):
    return 0.5 * jnp.tanh(0.5 * values) + 0.5


def per_hidden(weights):
    count = weights.shape[1]
    parts = [jnp.broadcast_to(weights[e : e + 1], (EFF, count)) for e in range(EXPERTS)]
    parts.append(jnp.broadcast_to(weights[EXPERTS : EXPERTS + 1], (SHARED, count)))
    return jnp.concatenate(parts, axis=0)


def routing(rows, inv_row, switch_mat):
    logits = dot_last(switch_mat, rows) * inv_row
    place = lax.broadcasted_iota(jnp.int32, logits.shape, 0)
    shown = jnp.where(place < EXPERTS, logits, NEG_BIG)
    powers = jnp.exp(shown - jnp.max(shown, axis=0, keepdims=True))
    probs = powers / jnp.sum(powers, axis=0, keepdims=True)
    return logits, jnp.where(place == EXPERTS, sigmoid(logits), probs)


def mean_square_inverse(rows):
    wide = rows.astype(f32)
    return lax.rsqrt(jnp.sum(wide * wide, axis=1, keepdims=True) * (1.0 / WIDTH) + EPSILON)


def attend_body(
    core_ref, own_ref, other_ref, w_ref, bias_ref, cos_ref, sin_ref, see_ref, w_out_ref,
    keep_ref, send_ref, rows_ref, cot_ref, inv_ref, plain_ref, qkv_ref, probs_ref, mixed_ref,
):
    core = core_ref[0]
    lay_rows(rows_ref, core, own_ref, other_ref)
    lay_rows(cot_ref, core, own_ref, other_ref, slice(ROWS, 2 * ROWS))
    rows = rows_ref[...]
    inverse = mean_square_inverse(rows)
    inv_ref[...] = jnp.broadcast_to(inverse, (ROWS, COLS))
    plain = dot_plain(rows, w_ref[...]) * inverse
    plain_ref[...] = plain
    biased = plain + bias_ref[...]
    cosine, sine_table = cos_ref[...], sin_ref[...]
    query = rotate(biased[:, :HDIM], cosine, sine_table).astype(bf16)
    keys = rotate(biased[:, HDIM : 2 * HDIM], cosine, sine_table).astype(bf16)
    values = biased[:, 2 * HDIM :].astype(bf16)
    qkv_ref[:, :HDIM] = query
    qkv_ref[:, HDIM : 2 * HDIM] = keys
    qkv_ref[:, 2 * HDIM :] = values
    scores = dot_last(query, keys) * SCALE
    masked = jnp.where(see_ref[...] > 0.5, scores, NEG_BIG)
    powers = jnp.exp(masked - jnp.max(masked, axis=1, keepdims=True))
    probs = powers / jnp.sum(powers, axis=1, keepdims=True)
    probs_ref[...] = probs
    mixed = dot_plain(probs.astype(bf16), values).astype(bf16)
    mixed_ref[...] = mixed
    part_chips(core, dot_plain(mixed, w_out_ref[...]), keep_ref, send_ref)


def start_body(tokens_ref, cot_ref, routes_ref, wide_ref, tall_ref, chosen_ref):
    tokens, cot = tokens_ref[...], cot_ref[...]
    place = lax.broadcasted_iota(jnp.int32, (8, ROWS), 0)
    routes = routes_ref[...]
    found = place >= EXPERTS
    for choice in range(routes.shape[0]):
        found = found | (place == routes[choice : choice + 1])
    chosen = jnp.where(found, 1.0, 0.0)
    chosen_ref[...] = chosen
    last = jnp.concatenate([chosen[:, 2 * COLS :], jnp.zeros((8, HALF), f32)], axis=1)
    shown = [chosen[:, :COLS], chosen[:, COLS : 2 * COLS], last, jnp.zeros((8, COLS), f32)]
    tall_ref[:ROWS] = cot
    tall_ref[ROWS:] = jnp.concatenate(shown, axis=0).astype(bf16)
    for chip in range(NCHIP):
        wide_ref[chip, :ROWS] = tokens
        wide_ref[chip, ROWS:] = cot


def residual_body(tokens_ref, arrived_ref, resid_ref, wide_ref, low_ref):
    total = tokens_ref[...].astype(f32)
    for chip in range(NCHIP):
        total = total + arrived_ref[chip].astype(f32)
    resid_ref[...] = total
    low = total.astype(bf16)
    low_ref[...] = low
    for chip in range(NCHIP):
        wide_ref[chip] = low


def plain_grad_body(rows_ref, down_ref, out_ref):
    out_ref[...] = dot_last(down_ref[...], rows_ref[...]).astype(bf16)


def experts_body(
    core_ref, own_ref, other_ref, chosen_ref, switch_ref, gate_ref, up_ref, plain_ref,
    keep_ref, send_ref, act_ref, extra_ref, rows_ref, inv_ref, inv_row_ref, probs_ref, logits_ref,
):
    core = core_ref[0]
    lay_rows(rows_ref, core, own_ref, other_ref)
    rows = rows_ref[...]
    inverse = mean_square_inverse(rows)
    inv_ref[...] = jnp.broadcast_to(inverse, (ROWS, COLS))
    inv_row = to_row(inverse)
    inv_row_ref[...] = inv_row
    logits, probs = routing(rows, inv_row, switch_ref[...])
    logits_ref[...] = logits
    probs_ref[...] = probs
    mixing = probs * chosen_ref[...]
    gate_val = dot_last(gate_ref[...], rows) * inv_row
    up_val = dot_last(up_ref[...], rows) * inv_row
    spread_mix = per_hidden(mixing)
    sigma = sigmoid(gate_val)
    silu = gate_val * sigma
    act = silu * up_val
    grad_plain = plain_ref[...].astype(f32)
    pair = act * grad_plain
    grad_act = spread_mix * grad_plain
    grad_gate = grad_act * up_val * (sigma + silu * (1.0 - sigma))
    grad_up = grad_act * silu
    sums = [
        jnp.sum(pair[e * EFF : (e + 1) * EFF], axis=0, keepdims=True) for e in range(EXPERTS)
    ]
    sums.append(jnp.sum(pair[ROUTED:], axis=0, keepdims=True))
    sums.append(jnp.sum(grad_gate * gate_val + grad_up * up_val, axis=0, keepdims=True))
    sums = jnp.concatenate(sums, axis=0)
    extra_ref[0] = sums[:, :COLS]
    extra_ref[1] = sums[:, COLS : 2 * COLS]
    extra_ref[2] = jnp.concatenate([sums[:, 2 * COLS :], jnp.zeros((8, HALF), f32)], axis=1)
    act_ref[...] = (spread_mix * act).astype(bf16)
    part = dot_first(grad_gate.astype(bf16), gate_ref[...])
    part = part + dot_first(grad_up.astype(bf16), up_ref[...])
    part_chips(core, part, keep_ref, send_ref)


def branches_body(act_ref, down_ref, out_ref):
    part = dot_first(act_ref[...], down_ref[...]).astype(bf16)
    for block in range(NTP):
        out_ref[block * ROWS : (block + 1) * ROWS] = part[:, block * COLS : (block + 1) * COLS]


def payload_body(keep_ref, came_ref, extra_ref, extra_came_ref, out_ref):
    extra = extra_ref[...] + extra_came_ref[...]
    high = extra.astype(bf16)
    low = (extra - high.astype(f32)).astype(bf16)
    for chip in range(NCHIP):
        out_ref[chip, :ROWS] = (
            keep_ref[chip].astype(f32) + came_ref[chip].astype(f32)
        ).astype(bf16)
        out_ref[chip, ROWS:] = jnp.concatenate([high, low], axis=0)


def second_norm_body(
    core_ref, arrived_ref, probs_ref, chosen_ref, logits_ref, inv_row_ref, switch_ref, cot_ref,
    resid_ref, inv_ref, gain_ref, wide_ref, grad_ref, router_ref, extra_ref,
):
    dn = arrived_ref[0, :ROWS].astype(f32)
    extra = arrived_ref[0, ROWS:].astype(f32)
    for chip in range(1, NCHIP):
        dn = dn + arrived_ref[chip, :ROWS].astype(f32)
        extra = extra + arrived_ref[chip, ROWS:].astype(f32)
    extra = extra[:EXTRA] + extra[EXTRA:]
    sums = jnp.concatenate([extra[:8], extra[8:16], extra[16:24]], axis=1)[:, :ROWS]
    place = lax.broadcasted_iota(jnp.int32, (8, ROWS), 0)
    probs = probs_ref[...]
    routed = place < EXPERTS
    weighed = jnp.where(routed, probs * (sums * chosen_ref[...]), 0.0)
    total = jnp.sum(weighed, axis=0, keepdims=True)
    low = jnp.where(routed, weighed - probs * total, sums * probs * (1.0 - probs))
    low = jnp.where(place <= EXPERTS, low, 0.0).astype(bf16)
    low_wide = low.astype(f32)
    router_ref[...] = (low_wide * inv_row_ref[...]).astype(bf16)
    dn = dn + dot_first(low, switch_ref[...])
    stat = sums[EXPERTS + 1 :] + jnp.sum(low_wide * logits_ref[...], axis=0, keepdims=True)
    inverse = inv_ref[...]
    normed = resid_ref[...].astype(bf16).astype(f32) * inverse
    own = jnp.sum(dn * normed, axis=0, keepdims=True) / gain_ref[...]
    first = core_ref[0] == 0
    spot = lax.broadcasted_iota(jnp.int32, (8, COLS), 0)
    extra_ref[...] = jnp.where(spot == jnp.where(first, 0, 1), own, 0.0)
    grad = inverse * (dn - normed * (to_columns(stat) * (1.0 / WIDTH)))
    grad = grad + cot_ref[...].astype(f32)
    grad_ref[...] = grad
    low_grad = grad.astype(bf16)
    for chip in range(NCHIP):
        wide_ref[chip] = low_grad


def attend_back_body(
    core_ref, own_ref, other_ref, w_out_ref, qkv_ref, probs_ref, plain_ref, inv_ref, cos_ref,
    sin_ref, w_ref, rows_ref, gain_own_ref,
    keep_ref, send_ref, extra_ref, grad_rows_ref, scaled_ref, bias_ref,
):
    core = core_ref[0]
    lay_rows(grad_rows_ref, core, own_ref, other_ref)
    grad_attn = grad_rows_ref[...]
    query, keys = qkv_ref[:, :HDIM], qkv_ref[:, HDIM : 2 * HDIM]
    values = qkv_ref[:, 2 * HDIM :]
    probs = probs_ref[...]
    heads = dot_last(grad_attn, w_out_ref[...]).astype(bf16)
    dprobs = dot_last(heads, values)
    dscores = probs * (dprobs - jnp.sum(probs * dprobs, axis=1, keepdims=True))
    dscores = dscores.astype(bf16)
    cosine, sine_table = cos_ref[...], -sin_ref[...]
    dq = rotate(dot_plain(dscores, keys) * SCALE, cosine, sine_table)
    dk = rotate(dot_first(dscores, query) * SCALE, cosine, sine_table)
    dv = dot_first(probs.astype(bf16), heads)
    d_low = jnp.concatenate([dq, dk, dv], axis=1).astype(bf16)
    d_wide = d_low.astype(f32)
    inverse = inv_ref[...]
    scaled_ref[...] = (d_wide * jnp.concatenate([inverse] * 3, axis=1)).astype(bf16)
    bias_ref[...] = jnp.sum(d_wide, axis=0, keepdims=True)
    part = dot_last(d_low, w_ref[...])
    part_chips(core, part, keep_ref, send_ref)
    rows = rows_ref[...]
    normed = rows.astype(f32) * inverse[:, :1]
    gains = jnp.sum(part * normed, axis=0, keepdims=True)
    for block in range(NTP):
        extra_ref[block : block + 1] = gains[:, block * COLS : (block + 1) * COLS]
    stat = to_row(jnp.sum(d_wide * plain_ref[...], axis=1, keepdims=True))
    stat = jnp.concatenate([stat, jnp.zeros((1, HALF), f32)], axis=1)
    for block in range(3):
        extra_ref[NTP + block : NTP + block + 1] = stat[:, block * COLS : (block + 1) * COLS]
    extra_ref[NTP + 3 :] = gain_own_ref[: EXTRA - NTP - 3]


def attend_weights_body(
    scaled_ref, bias_ref, rows_ref, mixed_ref, grad_rows_ref, router_ref, rows_two_ref, gain_two_ref,
    trees_ref, tail_ref,
):
    grad_w = dot_first(scaled_ref[...], rows_ref[...]).astype(bf16)
    grad_out = dot_first(mixed_ref[...], grad_rows_ref[...]).astype(bf16)
    for tree in range(NDP):
        trees_ref[tree, :QKV_CHUNK] = grad_w[tree * QKV_CHUNK : (tree + 1) * QKV_CHUNK]
        trees_ref[tree, QKV_CHUNK:] = grad_out[tree * OUT_CHUNK : (tree + 1) * OUT_CHUNK]
    bias = jnp.concatenate([bias_ref[...], jnp.zeros((1, WIDTH - QKV), f32)], axis=1)
    router = dot_plain(router_ref[...], rows_two_ref[...]) * gain_two_ref[...]
    place = lax.broadcasted_iota(jnp.int32, (8, WIDTH), 0)
    router = jnp.where(place == EXPERTS + 1, bias, router)
    tail_ref[...] = router


def first_norm_body(arrived_ref, tokens_ref, inv_ref, grad_res_ref, out_ref, small_ref):
    dn = arrived_ref[0, :ROWS].astype(f32)
    tails = [arrived_ref[chip, ROWS:].astype(f32) for chip in range(NCHIP)]
    for chip in range(1, NCHIP):
        dn = dn + arrived_ref[chip, :ROWS].astype(f32)
    tails = [tail[:EXTRA] + tail[EXTRA:] for tail in tails]
    extra = sum(tails[1:], tails[0])
    stat = jnp.concatenate([extra[NTP + k : NTP + k + 1] for k in range(3)], axis=1)
    stat = to_columns(stat)[:ROWS] * (1.0 / WIDTH)
    inverse = inv_ref[...]
    normed = tokens_ref[...].astype(f32) * inverse
    out_ref[...] = inverse * (dn - normed * stat) + grad_res_ref[...]
    small_ref[...] = jnp.zeros((8, WIDTH), f32)
    for block in range(NTP):
        spot = slice(block * COLS, (block + 1) * COLS)
        small_ref[0:1, spot] = extra[block : block + 1]
        place = NTP + 3 + block % 2
        small_ref[1:2, spot] = tails[block // 2][place : place + 1]


def trees_body(arrived_ref, tail_ref, small_ref, out_ref):
    total = arrived_ref[0].astype(f32)
    for tree in range(1, NDP):
        total = total + arrived_ref[tree].astype(f32)
    low = total.astype(bf16)
    tail = jnp.concatenate([tail_ref[...], small_ref[...]], axis=0).astype(bf16)
    for tree in range(NDP):
        out_ref[tree, : QKV_CHUNK + OUT_CHUNK] = low
        out_ref[tree, QKV_CHUNK + OUT_CHUNK :] = tail


def last_body(
    all_ref, gain_ref, resid_ref, ffn_ref, query_ref, key_ref, value_ref, out_ref, bias_q_ref,
    bias_k_ref, bias_v_ref, router_ref, switch_ref, one_ref, two_ref, output_ref,
):
    mats = jnp.concatenate([all_ref[tree, :QKV_CHUNK] for tree in range(NDP)], axis=0)
    mats = mats.astype(f32) * gain_ref[...]
    query_ref[...] = jnp.transpose(mats[:HDIM])
    key_ref[...] = jnp.transpose(mats[HDIM : 2 * HDIM])
    value_ref[...] = jnp.transpose(mats[2 * HDIM :])
    start = QKV_CHUNK + OUT_CHUNK
    tail = jnp.zeros((16, WIDTH), f32)
    for tree in range(NDP):
        out_ref[tree * OUT_CHUNK : (tree + 1) * OUT_CHUNK] = all_ref[
            tree, QKV_CHUNK:start
        ].astype(f32)
        tail = tail + all_ref[tree, start:].astype(f32)
    router_ref[...] = tail[:EXPERTS]
    switch_ref[...] = tail[EXPERTS : EXPERTS + 1]
    bias = tail[EXPERTS + 1 : EXPERTS + 2]
    bias_q_ref[...] = bias[:, :HDIM]
    bias_k_ref[...] = bias[:, HDIM : 2 * HDIM]
    bias_v_ref[...] = bias[:, 2 * HDIM : QKV]
    one_ref[...] = tail[8:9] / gain_ref[...]
    two_ref[...] = tail[9:10]
    output_ref[...] = (resid_ref[...] + ffn_ref[...].astype(f32)).astype(bf16)


def lay_trees(rows_ref, blocks_ref, trees):
    for tree in range(trees):
        for block in range(NTP):
            rows_ref[tree * ROWS : (tree + 1) * ROWS, block * COLS : (block + 1) * COLS] = (
                blocks_ref[tree, block]
            )


def plain_all_body(blocks_ref, down_ref, *refs):
    out_ref, rows_ref = refs[-2:]
    lay_trees(rows_ref, blocks_ref, 2)
    out_ref[...] = dot_last(down_ref[...], rows_ref[...]).astype(bf16)


BLOCK = 512
READY = ((0, 1), (2, 3), (4,), (5, 6), (7,))


def hidden_all_body(
    blocks_ref, plain_ref, chosen_ref, switch_ref, gate_ref, up_ref,
    grad_gate_ref, grad_up_ref, act_ref, rows_ref, sems,
):

    def copy(tree, block):
        where = slice(tree * ROWS, (tree + 1) * ROWS), slice(block * COLS, (block + 1) * COLS)
        return pltpu.make_async_copy(
            blocks_ref.at[tree, block, :ROWS], rows_ref.at[where], sems.at[tree, block]
        )

    step = pl.program_id(0)

    @pl.when(step == 0)
    def _():
        for tree in range(NDP):
            for block in range(NTP):
                copy(tree, block).start()

    for number, trees in enumerate(READY):

        @pl.when(step == number)
        def _(trees=trees):
            for tree in trees:
                for block in range(NTP):
                    copy(tree, block).wait()

    rows = rows_ref[pl.ds(pl.multiple_of(step * BLOCK, BLOCK), BLOCK), :]
    inverse = to_row(mean_square_inverse(rows))
    _, probs = routing(rows, inverse, switch_ref[...])
    mix = probs * chosen_ref[...]
    half = dot_last(gate_ref[...], rows) * (0.5 * inverse)
    up_val = dot_last(up_ref[...], rows)
    twice = jnp.tanh(half) + 1.0
    silu = half * twice
    weight = per_hidden(mix * inverse)
    act_ref[...] = (weight * (silu * up_val)).astype(bf16)
    grad_act = weight * plain_ref[...].astype(f32)
    grad_up_ref[...] = (grad_act * silu).astype(bf16)
    slope = twice + silu * (2.0 - twice)
    grad_gate_ref[...] = (grad_act * (up_val * (0.5 * inverse)) * slope).astype(bf16)


def weights_body(
    grad_gate_ref, grad_up_ref, act_ref, resid_ref, cot_ref, gain_ref,
    gate_r_ref, gate_s_ref, up_r_ref, up_s_ref, down_r_ref, down_s_ref,
):
    def columns(ref):
        blocks = [ref[:, k].reshape(ALL_ROWS, COLS) for k in range(ref.shape[1])]
        return jnp.concatenate(blocks, axis=1)

    resid = columns(resid_ref)
    gain = gain_ref[...]
    grad = dot_plain(grad_gate_ref[...], resid) * gain
    gate_r_ref[...] = grad[:ROUTED]
    gate_s_ref[...] = grad[ROUTED:]
    grad = dot_plain(grad_up_ref[...], resid) * gain
    up_r_ref[...] = grad[:ROUTED]
    up_s_ref[...] = grad[ROUTED:]
    grad = dot_plain(act_ref[...], columns(cot_ref))
    down_r_ref[...] = grad[:ROUTED]
    down_s_ref[...] = grad[ROUTED:]


def once(shape):
    zero = (0,) * len(shape)
    return pl.BlockSpec(shape, lambda i: zero, pipeline_mode=pl.Buffered(1))


PAIR = 2 * ROWS
PAIR_FLOPS = 2 * HIDDEN * WIDTH * ALL_ROWS


def plain_all(blocks, down_mat, first, held):
    held = [] if held is None else [held]
    return pl.pallas_call(
        plain_all_body,
        grid=(NDP // 4,),
        in_specs=[
            pl.BlockSpec((2, NTP, ROWS, COLS), lambda i: (first + i, 0, 0, 0)),
            once((HIDDEN, WIDTH)),
        ]
        + [pl.BlockSpec(memory_space=pltpu.HBM)] * len(held),
        out_specs=pl.BlockSpec((HIDDEN, PAIR), lambda i: (0, first + i)),
        out_shape=sds((HIDDEN, ALL_ROWS), bf16),
        scratch_shapes=[pltpu.VMEM((PAIR, WIDTH), bf16)],
        input_output_aliases={2: 0} if held else {},
        compiler_params=pltpu.CompilerParams(vmem_limit_bytes=60 * MIB),
        cost_estimate=pl.CostEstimate(
            flops=PAIR_FLOPS // 2, bytes_accessed=14 * MIB, transcendentals=0
        ),
    )(blocks, down_mat, *held)


def hidden_all(blocks, plain, chosen, switch_mat, gate_mat, up_mat):
    return pl.pallas_call(
        hidden_all_body,
        grid=(ALL_ROWS // BLOCK,),
        in_specs=[
            pl.BlockSpec(memory_space=pltpu.HBM),
            pl.BlockSpec((HIDDEN, BLOCK), lambda i: (0, i)),
            pl.BlockSpec((8, BLOCK), lambda i: (0, i)),
            once((8, WIDTH)),
            once((HIDDEN, WIDTH)),
            once((HIDDEN, WIDTH)),
        ],
        out_specs=[pl.BlockSpec((HIDDEN, BLOCK), lambda i: (0, i))] * 3,
        out_shape=[sds((HIDDEN, ALL_ROWS), bf16)] * 3,
        scratch_shapes=[
            pltpu.VMEM((ALL_ROWS, WIDTH), bf16),
            pltpu.SemaphoreType.DMA((NDP, NTP)),
        ],
        compiler_params=pltpu.CompilerParams(vmem_limit_bytes=60 * MIB),
        cost_estimate=pl.CostEstimate(
            flops=2 * PAIR_FLOPS, bytes_accessed=40 * MIB, transcendentals=HIDDEN * ALL_ROWS
        ),
    )(blocks, plain, chosen, switch_mat, gate_mat, up_mat)


WIDE = 2


def weight_grads(grad_gate, grad_up, act, resid, cot, gain):
    step = WIDE * COLS
    wide = pl.BlockSpec((NDP, WIDE, ROWS, COLS), lambda i: (0, i, 0, 0))
    return pl.pallas_call(
        weights_body,
        grid=(WIDTH // step,),
        in_specs=[
            once((HIDDEN, ALL_ROWS)),
            once((HIDDEN, ALL_ROWS)),
            once((HIDDEN, ALL_ROWS)),
            wide,
            wide,
            pl.BlockSpec((1, step), lambda i: (0, i)),
        ],
        out_specs=[
            pl.BlockSpec((ROUTED, step), lambda i: (0, i)),
            pl.BlockSpec((SHARED, step), lambda i: (0, i)),
        ]
        * 3,
        out_shape=[sds((ROUTED, WIDTH), f32), sds((SHARED, WIDTH), f32)] * 3,
        compiler_params=pltpu.CompilerParams(vmem_limit_bytes=60 * MIB),
        cost_estimate=pl.CostEstimate(
            flops=3 * PAIR_FLOPS, bytes_accessed=56 * MIB, transcendentals=0
        ),
    )(grad_gate, grad_up, act, resid, cot, gain)


def widen(block, count):
    return jnp.broadcast_to(block[None], (count,) + block.shape)


def over_chips(blocks):
    return lax.all_to_all(blocks, CHIPS, 0, 0)


def over_trees(blocks):
    return lax.all_to_all(blocks, TREES, 0, 0)


def after(value, *others):
    return lax.optimization_barrier((value,) + others)[0]


def swap(block):
    return lax.ppermute(block, "core", SWAP)


def on_device(
    tokens,
    cotangent,
    routes,
    segments,
    parents,
    positions,
    norm_one,
    w_query,
    b_query,
    w_key,
    b_key,
    w_value,
    b_value,
    w_out,
    norm_two,
    router,
    expert_gate,
    expert_up,
    expert_down,
    shared_gate,
    shared_up,
    shared_down,
    shared_switch,
):
    core = lax.axis_index("core").astype(jnp.int32).reshape(1)
    col_start = lax.axis_index(TENSOR) * COLS
    gain_one = norm_one.astype(f32)
    gain_two = norm_two.astype(f32)

    def to_hidden(routed, shared):
        mat = jnp.concatenate(
            [jnp.transpose(routed, (0, 2, 1)).reshape(ROUTED, WIDTH), shared.T], axis=0
        )
        return (mat.astype(f32) * gain_two).astype(bf16)

    gate_mat = to_hidden(expert_gate, shared_gate)
    up_mat = to_hidden(expert_up, shared_up)
    down_mat = jnp.concatenate([expert_down.reshape(ROUTED, WIDTH), shared_down], axis=0)
    w_qkv = jnp.concatenate([w_query, w_key, w_value], axis=1)
    w_qkv = (w_qkv.astype(f32) * gain_one[:, None]).astype(bf16)
    bias = jnp.concatenate([b_query, b_key, b_value]).astype(f32)[None]
    switch_mat = jnp.concatenate(
        [router.T, shared_switch[None], jnp.zeros((1, WIDTH), bf16)], axis=0
    )
    switch_mat = (switch_mat.astype(f32) * gain_two).astype(bf16)
    switch_cols = lax.dynamic_slice_in_dim(switch_mat, col_start, COLS, 1)
    gain_two_cols = lax.dynamic_slice_in_dim(gain_two, col_start, COLS, 0)[None]
    frequency = jnp.power(THETA, -2.0 * jnp.arange(HALF, dtype=f32) / HDIM)
    angles = positions.astype(f32)[:, None] * frequency[None, :]
    cosine = jnp.cos(angles)
    sine_table = jnp.sin(angles)
    visible = (
        (segments[None, :] == 0)
        | (segments[None, :] == segments[:, None])
        | (segments[None, :] == parents[:, None])
    ) & (positions[None, :] <= positions[:, None])
    visible = visible.astype(f32)
    wide, tall, chosen = call(
        start_body,
        [
            sds((NCHIP, 2 * ROWS, COLS), bf16), sds((ROWS + SHOWN, COLS), bf16),
            sds((8, ROWS), f32),
        ],
        [tokens, cotangent, routes.T],
        moved=2 * MIB, limit=16,
    )
    own = over_chips(wide)
    own = after(own, gate_mat, up_mat, down_mat, w_qkv, bias, cosine, sine_table, visible)
    cot_blocks = lax.all_gather(tall, TREES + TENSOR, axis=0)
    cot_blocks = cot_blocks.reshape(NDP, NTP, ROWS + SHOWN, COLS)
    chosen_all = cot_blocks[:, 0, ROWS : ROWS + EXTRA].reshape(NDP, 3, 8, COLS)
    chosen_all = jnp.transpose(chosen_all, (2, 0, 1, 3)).reshape(8, NDP, 3 * COLS)
    chosen_all = chosen_all[:, :, :ROWS].reshape(8, ALL_ROWS).astype(f32)
    other = swap(own)
    blocks8 = (NCHIP, ROWS, COLS)
    keep, send, rows_one, cot_rows, inv_one, plain, qkv, probs, mixed = call(
        attend_body,
        [
            sds(blocks8, bf16), sds(blocks8, bf16), sds((ROWS, WIDTH), bf16),
            sds((ROWS, WIDTH), bf16), sds((ROWS, COLS), f32), sds((ROWS, QKV), f32), sds((ROWS, QKV), bf16),
            sds((ROWS, ROWS), f32), sds((ROWS, HDIM), bf16),
        ],
        [core, own, other, w_qkv, bias, cosine, sine_table, visible, w_out],
        smem=1, flops=900_000_000, moved=8 * MIB,
    )
    arrived = over_chips((keep.astype(f32) + swap(send).astype(f32)).astype(bf16))
    grad_plain = call(
        plain_grad_body,
        [sds((HIDDEN, ROWS), bf16)],
        [cot_rows, down_mat],
        flops=2 * HIDDEN * WIDTH * ROWS, moved=6 * MIB,
    )[0]
    resid_cols, wide, low = call(
        residual_body,
        [sds((ROWS, COLS), f32), sds(blocks8, bf16), sds((ROWS, COLS), bf16)],
        [tokens, after(arrived, grad_plain)],
        moved=2 * MIB,
    )

    own = over_chips(wide)
    resid_blocks = lax.all_gather(low, TREES + TENSOR, axis=0)
    resid_blocks = resid_blocks.reshape(NDP, NTP, ROWS, COLS)
    (
        keep, send, act, extra, rows_two, inv_two, inv_row, gates, logits,
    ) = call(
        experts_body,
        [
            sds(blocks8, bf16), sds(blocks8, bf16), sds((HIDDEN, ROWS), bf16),
            sds((3, 8, COLS), f32), sds((ROWS, WIDTH), bf16), sds((ROWS, COLS), f32),
            sds((1, ROWS), f32), sds((8, ROWS), f32), sds((8, ROWS), f32),
        ],
        [core, own, swap(own), chosen, switch_mat, gate_mat, up_mat, grad_plain],
        smem=1, flops=8 * HIDDEN * WIDTH * ROWS,
        moved=20 * MIB,
    )
    extra = extra.reshape(EXTRA, COLS)
    payload = call(
        payload_body,
        [sds((NCHIP, SENT, COLS), bf16)],
        [keep, swap(send), extra, swap(extra)],
        moved=4 * MIB, limit=16,
    )[0]
    arrived = over_chips(payload)
    plain_half = plain_all(cot_blocks, down_mat, 0, None)
    wide, grad_res, router_low, gain_own = call(
        second_norm_body,
        [
            sds(blocks8, bf16), sds((ROWS, COLS), f32), sds((8, ROWS), bf16),
            sds((8, COLS), f32),
        ],
        [
            core, after(arrived, plain_half), gates, chosen, logits, inv_row, switch_cols, cotangent,
            resid_cols,
            inv_two, gain_two_cols,
        ],
        smem=1, moved=3 * MIB,
    )
    own = over_chips(wide)
    ffn = call(
        branches_body,
        [sds((NTP * ROWS, COLS), bf16)],
        [after(act, grad_res), down_mat],
        flops=2 * HIDDEN * WIDTH * ROWS, moved=8 * MIB,
    )[0]
    plain_rows = plain_all(cot_blocks, down_mat, 2, after(plain_half, grad_res))
    own = after(own, ffn, plain_rows)
    keep, send, extra, grad_rows, scaled, bias_sum = call(
        attend_back_body,
        [
            sds(blocks8, bf16), sds(blocks8, bf16), sds((EXTRA, COLS), f32),
            sds((ROWS, WIDTH), bf16), sds((ROWS, QKV), bf16), sds((1, QKV), f32),
        ],
        [
            core, own, swap(own), w_out, qkv, probs, plain, inv_one, cosine, sine_table, w_qkv,
            rows_one, gain_own,
        ],
        smem=1, flops=1_000_000_000,
        moved=10 * MIB,
    )
    payload = call(
        payload_body,
        [sds((NCHIP, SENT, COLS), bf16)],
        [keep, swap(send), extra, swap(extra)],
        moved=4 * MIB, limit=16,
    )[0]
    arrived = over_chips(payload)
    trees, tail = call(
        attend_weights_body,
        [sds((NDP, QKV_CHUNK + OUT_CHUNK, WIDTH), bf16), sds((8, WIDTH), f32)],
        [
            after(scaled, payload), bias_sum, rows_one, mixed, grad_rows, router_low, rows_two,
            gain_two[None],
        ],
        flops=1_000_000_000, moved=8 * MIB,
    )
    tree_sums = over_trees(trees)
    grads = hidden_all(
        after(resid_blocks, payload), plain_rows, chosen_all, switch_mat, gate_mat, up_mat
    )
    ffn = lax.psum_scatter(
        after(ffn, resid_blocks, payload), TENSOR, scatter_dimension=0, tiled=True
    )
    input_grad, small = call(
        first_norm_body,
        [sds((ROWS, COLS), f32), sds((8, WIDTH), f32)],
        [arrived, tokens, inv_one, grad_res],
        moved=2 * MIB, limit=24,
    )
    chunk = QKV_CHUNK + OUT_CHUNK
    wide = call(
        trees_body,
        [sds((NDP, chunk + 16, WIDTH), bf16)],
        [after(tree_sums, *grads), tail, small],
        moved=6 * MIB, limit=24,
    )[0]
    everything = over_trees(wide)
    (
        grad_query, grad_key, grad_value, grad_out_proj, query_bias, key_bias, value_bias,
        grad_router, grad_switch, gain_one_sum, gain_two_sum, output,
    ) = call(
        last_body,
        [
            sds((WIDTH, HDIM), f32), sds((WIDTH, HDIM), f32), sds((WIDTH, HDIM), f32),
            sds((HDIM, WIDTH), f32), sds((1, HDIM), f32), sds((1, HDIM), f32),
            sds((1, HDIM), f32), sds((EXPERTS, WIDTH), f32), sds((1, WIDTH), f32),
            sds((1, WIDTH), f32), sds((1, WIDTH), f32), sds((ROWS, COLS), bf16),
        ],
        [everything, gain_one[None], resid_cols, ffn],
        moved=7 * MIB, limit=24,
    )

    gate_r, gate_s, up_r, up_s, down_r, down_s = weight_grads(
        after(grads[0], wide, input_grad), *grads[1:], resid_blocks, cot_blocks, gain_two[None]
    )

    def routed_cols(mat):
        return jnp.transpose(mat.reshape(EXPERTS, EFF, WIDTH), (0, 2, 1))

    return (
        output,
        input_grad,
        gain_one_sum.reshape(-1),
        grad_query,
        query_bias.reshape(-1),
        grad_key,
        key_bias.reshape(-1),
        grad_value,
        value_bias.reshape(-1),
        grad_out_proj,
        gain_two_sum.reshape(-1),
        grad_router.T,
        routed_cols(gate_r),
        routed_cols(up_r),
        down_r.reshape(EXPERTS, EFF, WIDTH),
        gate_s.T,
        up_s.T,
        down_s,
        grad_switch.reshape(-1),
    )


def solution(mesh):
    fine = Mesh(mesh.devices.reshape(4, 2, 2, 4, 2), TREES + TENSOR)
    both = P(TREES, TENSOR)
    cols = P(None, TENSOR)
    placed = (
        both,
        both,
        P(TREES, None),
        P(TREES),
        P(TREES),
        P(TREES),
        P(),
        cols,
        P(TENSOR),
        cols,
        P(TENSOR),
        cols,
        P(TENSOR),
        P(TENSOR, None),
        P(),
        P(),
        P(None, None, TENSOR),
        P(None, None, TENSOR),
        P(None, TENSOR, None),
        cols,
        cols,
        P(TENSOR, None),
        P(),
    )
    return jax.shard_map(
        on_device,
        mesh=fine,
        in_specs=placed,
        out_specs=(
            both,
            both,
            P(),
            cols,
            P(TENSOR),
            cols,
            P(TENSOR),
            cols,
            P(TENSOR),
            P(TENSOR, None),
            P(),
            P(),
            P(None, None, TENSOR),
            P(None, None, TENSOR),
            P(None, TENSOR, None),
            cols,
            cols,
            P(TENSOR, None),
            P(),
        ),
        check_vma=False,
    )
```

```python
import functools

import jax
import jax.numpy as jnp
from jax import lax
from jax.experimental import pallas as pl
from jax.experimental.pallas import tpu as pltpu
from jax.sharding import Mesh
from jax.sharding import PartitionSpec as P

HDIM = 128
HALF = HDIM // 2
EPSILON = 1e-06
THETA = 1000000.0
NEG_BIG = -1e30
TREES = ("z", "xhi")
CHIPS = ("xlo", "y")
TENSOR = ("xlo", "y", "core")
SWAP = [(0, 1), (1, 0)]
NDP = 8
NCHIP = 8
NTP = 16
ROWS = 320
COLS = 128
WIDTH = 2048
EXPERTS = 6
EFF = 88
ROUTED = EXPERTS * EFF
SHARED = 352
HIDDEN = ROUTED + SHARED
ALL_ROWS = NDP * ROWS
EXTRA = 24
SHOWN = 32
TALL = 2 * ROWS + SHOWN
SENT = ROWS + 2 * EXTRA
QKV = 3 * HDIM
OUT_CHUNK = HDIM // NDP
QKV_CHUNK = QKV // NDP
SCALE = HDIM ** (-0.5)
f32 = jnp.float32
bf16 = jnp.bfloat16
MIB = 1024 * 1024


def dot_plain(left_mat, right_mat):
    return jnp.dot(left_mat, right_mat, preferred_element_type=f32)


def dot_last(left_mat, right_mat):
    return lax.dot_general(
        left_mat, right_mat, (((1,), (1,)), ((), ())), preferred_element_type=f32
    )


def dot_first(left_mat, right_mat):
    return lax.dot_general(
        left_mat, right_mat, (((0,), (0,)), ((), ())), preferred_element_type=f32
    )


def sds(shape, dtype):
    return jax.ShapeDtypeStruct(shape, dtype)


def call(body, out_shape, args, *, smem=0, flops=0, moved=0, limit=60):
    specs = [pl.BlockSpec(memory_space=pltpu.SMEM)] * smem
    specs += [pl.BlockSpec(memory_space=pltpu.VMEM)] * (len(args) - smem)
    return pl.pallas_call(
        body,
        in_specs=specs,
        out_specs=[pl.BlockSpec(memory_space=pltpu.VMEM)] * len(out_shape),
        out_shape=out_shape,
        compiler_params=pltpu.CompilerParams(vmem_limit_bytes=limit * MIB),
        cost_estimate=pl.CostEstimate(flops=flops, bytes_accessed=moved, transcendentals=0),
    )(*args)


def lay_rows(rows_ref, core, own_ref, other_ref, window=slice(0, ROWS)):
    for chip in range(NCHIP):
        own = pl.multiple_of((2 * chip + core) * COLS, COLS)
        other = pl.multiple_of((2 * chip + 1 - core) * COLS, COLS)
        rows_ref[:, pl.ds(own, COLS)] = own_ref[chip, window]
        rows_ref[:, pl.ds(other, COLS)] = other_ref[chip, window]


def part_chips(core, part, keep_ref, send_ref):
    first = core == 0
    for chip in range(NCHIP):
        even = part[:, 2 * chip * COLS : (2 * chip + 1) * COLS]
        odd = part[:, (2 * chip + 1) * COLS : (2 * chip + 2) * COLS]
        keep_ref[chip] = jnp.where(first, even, odd).astype(keep_ref.dtype)
        send_ref[chip] = jnp.where(first, odd, even).astype(send_ref.dtype)


def rotate(rows, cosine, sine_table):
    first, second = rows[:, :HALF], rows[:, HALF:]
    return jnp.concatenate(
        [first * cosine - second * sine_table, second * cosine + first * sine_table], axis=1
    )


def to_row(column):
    return jnp.transpose(jnp.broadcast_to(column, (column.shape[0], COLS)))[:1]


def to_columns(row):
    return jnp.transpose(jnp.broadcast_to(row, (COLS, row.shape[1])))


def sigmoid(values):
    return 0.5 * jnp.tanh(0.5 * values) + 0.5


def per_hidden(weights):
    count = weights.shape[1]
    parts = [jnp.broadcast_to(weights[e : e + 1], (EFF, count)) for e in range(EXPERTS)]
    parts.append(jnp.broadcast_to(weights[EXPERTS : EXPERTS + 1], (SHARED, count)))
    return jnp.concatenate(parts, axis=0)


def routing(rows, inv_row, switch_mat):
    logits = dot_last(switch_mat, rows) * inv_row
    place = lax.broadcasted_iota(jnp.int32, logits.shape, 0)
    shown = jnp.where(place < EXPERTS, logits, NEG_BIG)
    powers = jnp.exp(shown - jnp.max(shown, axis=0, keepdims=True))
    probs = powers / jnp.sum(powers, axis=0, keepdims=True)
    return logits, jnp.where(place == EXPERTS, sigmoid(logits), probs)


def mean_square_inverse(rows):
    wide = rows.astype(f32)
    return lax.rsqrt(jnp.sum(wide * wide, axis=1, keepdims=True) * (1.0 / WIDTH) + EPSILON)


def attend_body(
    core_ref, own_ref, other_ref, w_ref, bias_ref, cos_ref, sin_ref, see_ref, w_out_ref,
    keep_ref, send_ref, rows_ref, inv_ref, plain_ref, qkv_ref, probs_ref, mixed_ref,
):
    core = core_ref[0]
    lay_rows(rows_ref, core, own_ref, other_ref)
    rows = rows_ref[...]
    inverse = mean_square_inverse(rows)
    inv_ref[...] = jnp.broadcast_to(inverse, (ROWS, COLS))
    plain = dot_plain(rows, w_ref[...]) * inverse
    plain_ref[...] = plain
    biased = plain + bias_ref[...]
    cosine, sine_table = cos_ref[...], sin_ref[...]
    query = rotate(biased[:, :HDIM], cosine, sine_table).astype(bf16)
    keys = rotate(biased[:, HDIM : 2 * HDIM], cosine, sine_table).astype(bf16)
    values = biased[:, 2 * HDIM :].astype(bf16)
    qkv_ref[:, :HDIM] = query
    qkv_ref[:, HDIM : 2 * HDIM] = keys
    qkv_ref[:, 2 * HDIM :] = values
    scores = dot_last(query, keys) * SCALE
    masked = jnp.where(see_ref[...] > 0.5, scores, NEG_BIG)
    powers = jnp.exp(masked - jnp.max(masked, axis=1, keepdims=True))
    probs = powers / jnp.sum(powers, axis=1, keepdims=True)
    probs_ref[...] = probs
    mixed = dot_plain(probs.astype(bf16), values).astype(bf16)
    mixed_ref[...] = mixed
    part_chips(core, dot_plain(mixed, w_out_ref[...]), keep_ref, send_ref)


def start_body(tokens_ref, routes_ref, wide_ref, shown_ref, chosen_ref):
    tokens = tokens_ref[...]
    place = lax.broadcasted_iota(jnp.int32, (8, ROWS), 0)
    routes = routes_ref[...]
    found = place >= EXPERTS
    for choice in range(routes.shape[0]):
        found = found | (place == routes[choice : choice + 1])
    chosen = jnp.where(found, 1.0, 0.0)
    chosen_ref[...] = chosen
    last = jnp.concatenate([chosen[:, 2 * COLS :], jnp.zeros((8, HALF), f32)], axis=1)
    shown = [chosen[:, :COLS], chosen[:, COLS : 2 * COLS], last, jnp.zeros((8, COLS), f32)]
    shown_ref[...] = jnp.concatenate(shown, axis=0).astype(bf16)
    for chip in range(NCHIP):
        wide_ref[chip] = tokens


def residual_body(
    tokens_ref, arrived_ref, cot_ref, shown_ref, resid_ref, wide_ref, tall_ref
):
    total = tokens_ref[...].astype(f32)
    for chip in range(NCHIP):
        total = total + arrived_ref[chip].astype(f32)
    resid_ref[...] = total
    low = total.astype(bf16)
    tall_ref[:ROWS] = low
    tall_ref[ROWS : 2 * ROWS] = cot_ref[...]
    tall_ref[2 * ROWS :] = shown_ref[...]
    for chip in range(NCHIP):
        wide_ref[chip] = low


def plain_grad_body(rows_ref, down_ref, out_ref):
    out_ref[...] = dot_last(down_ref[...], rows_ref[...]).astype(bf16)


def experts_body(
    core_ref, own_ref, other_ref, chosen_ref, switch_ref, gate_ref, up_ref, plain_ref,
    keep_ref, send_ref, act_ref, extra_ref, rows_ref, inv_ref, inv_row_ref, probs_ref, logits_ref,
):
    core = core_ref[0]
    lay_rows(rows_ref, core, own_ref, other_ref)
    rows = rows_ref[...]
    inverse = mean_square_inverse(rows)
    inv_ref[...] = jnp.broadcast_to(inverse, (ROWS, COLS))
    inv_row = to_row(inverse)
    inv_row_ref[...] = inv_row
    logits, probs = routing(rows, inv_row, switch_ref[...])
    logits_ref[...] = logits
    probs_ref[...] = probs
    mixing = probs * chosen_ref[...]
    gate_val = dot_last(gate_ref[...], rows) * inv_row
    up_val = dot_last(up_ref[...], rows) * inv_row
    spread_mix = per_hidden(mixing)
    sigma = sigmoid(gate_val)
    silu = gate_val * sigma
    act = silu * up_val
    grad_plain = plain_ref[...].astype(f32)
    pair = act * grad_plain
    grad_act = spread_mix * grad_plain
    grad_gate = grad_act * up_val * (sigma + silu * (1.0 - sigma))
    grad_up = grad_act * silu
    sums = [
        jnp.sum(pair[e * EFF : (e + 1) * EFF], axis=0, keepdims=True) for e in range(EXPERTS)
    ]
    sums.append(jnp.sum(pair[ROUTED:], axis=0, keepdims=True))
    sums.append(jnp.sum(grad_gate * gate_val + grad_up * up_val, axis=0, keepdims=True))
    sums = jnp.concatenate(sums, axis=0)
    extra_ref[0] = sums[:, :COLS]
    extra_ref[1] = sums[:, COLS : 2 * COLS]
    extra_ref[2] = jnp.concatenate([sums[:, 2 * COLS :], jnp.zeros((8, HALF), f32)], axis=1)
    act_ref[...] = (spread_mix * act).astype(bf16)
    part = dot_first(grad_gate.astype(bf16), gate_ref[...])
    part = part + dot_first(grad_up.astype(bf16), up_ref[...])
    part_chips(core, part, keep_ref, send_ref)


def branches_body(act_ref, down_ref, out_ref):
    part = dot_first(act_ref[...], down_ref[...]).astype(bf16)
    for block in range(NTP):
        out_ref[block * ROWS : (block + 1) * ROWS] = part[:, block * COLS : (block + 1) * COLS]


def payload_body(keep_ref, came_ref, extra_ref, extra_came_ref, out_ref):
    extra = extra_ref[...] + extra_came_ref[...]
    high = extra.astype(bf16)
    low = (extra - high.astype(f32)).astype(bf16)
    for chip in range(NCHIP):
        out_ref[chip, :ROWS] = (
            keep_ref[chip].astype(f32) + came_ref[chip].astype(f32)
        ).astype(bf16)
        out_ref[chip, ROWS:] = jnp.concatenate([high, low], axis=0)


def second_norm_body(
    core_ref, arrived_ref, probs_ref, chosen_ref, logits_ref, inv_row_ref, switch_ref, cot_ref,
    resid_ref, inv_ref, gain_ref, wide_ref, grad_ref, router_ref, extra_ref,
):
    dn = arrived_ref[0, :ROWS].astype(f32)
    extra = arrived_ref[0, ROWS:].astype(f32)
    for chip in range(1, NCHIP):
        dn = dn + arrived_ref[chip, :ROWS].astype(f32)
        extra = extra + arrived_ref[chip, ROWS:].astype(f32)
    extra = extra[:EXTRA] + extra[EXTRA:]
    sums = jnp.concatenate([extra[:8], extra[8:16], extra[16:24]], axis=1)[:, :ROWS]
    place = lax.broadcasted_iota(jnp.int32, (8, ROWS), 0)
    probs = probs_ref[...]
    routed = place < EXPERTS
    weighed = jnp.where(routed, probs * (sums * chosen_ref[...]), 0.0)
    total = jnp.sum(weighed, axis=0, keepdims=True)
    low = jnp.where(routed, weighed - probs * total, sums * probs * (1.0 - probs))
    low = jnp.where(place <= EXPERTS, low, 0.0).astype(bf16)
    low_wide = low.astype(f32)
    router_ref[...] = (low_wide * inv_row_ref[...]).astype(bf16)
    dn = dn + dot_first(low, switch_ref[...])
    stat = sums[EXPERTS + 1 :] + jnp.sum(low_wide * logits_ref[...], axis=0, keepdims=True)
    inverse = inv_ref[...]
    normed = resid_ref[...].astype(bf16).astype(f32) * inverse
    own = jnp.sum(dn * normed, axis=0, keepdims=True) / gain_ref[...]
    first = core_ref[0] == 0
    spot = lax.broadcasted_iota(jnp.int32, (8, COLS), 0)
    extra_ref[...] = jnp.where(spot == jnp.where(first, 0, 1), own, 0.0)
    grad = inverse * (dn - normed * (to_columns(stat) * (1.0 / WIDTH)))
    grad = grad + cot_ref[...].astype(f32)
    grad_ref[...] = grad
    low_grad = grad.astype(bf16)
    for chip in range(NCHIP):
        wide_ref[chip] = low_grad


def attend_back_body(
    core_ref, own_ref, other_ref, w_out_ref, qkv_ref, probs_ref, plain_ref, inv_ref, cos_ref,
    sin_ref, w_ref, rows_ref, gain_own_ref, mixed_ref, router_ref, rows_two_ref, gain_two_ref,
    keep_ref, send_ref, extra_ref, trees_ref, tail_ref, grad_rows_ref,
):
    core = core_ref[0]
    lay_rows(grad_rows_ref, core, own_ref, other_ref)
    grad_attn = grad_rows_ref[...]
    query, keys = qkv_ref[:, :HDIM], qkv_ref[:, HDIM : 2 * HDIM]
    values = qkv_ref[:, 2 * HDIM :]
    probs = probs_ref[...]
    heads = dot_last(grad_attn, w_out_ref[...]).astype(bf16)
    dprobs = dot_last(heads, values)
    dscores = probs * (dprobs - jnp.sum(probs * dprobs, axis=1, keepdims=True))
    dscores = dscores.astype(bf16)
    cosine, sine_table = cos_ref[...], -sin_ref[...]
    dq = rotate(dot_plain(dscores, keys) * SCALE, cosine, sine_table)
    dk = rotate(dot_first(dscores, query) * SCALE, cosine, sine_table)
    dv = dot_first(probs.astype(bf16), heads)
    d_low = jnp.concatenate([dq, dk, dv], axis=1).astype(bf16)
    d_wide = d_low.astype(f32)
    inverse = inv_ref[...]
    scaled = (d_wide * jnp.concatenate([inverse] * 3, axis=1)).astype(bf16)
    part = dot_last(d_low, w_ref[...])
    part_chips(core, part, keep_ref, send_ref)
    rows = rows_ref[...]
    normed = rows.astype(f32) * inverse[:, :1]
    gains = jnp.sum(part * normed, axis=0, keepdims=True)
    for block in range(NTP):
        extra_ref[block : block + 1] = gains[:, block * COLS : (block + 1) * COLS]
    stat = to_row(jnp.sum(d_wide * plain_ref[...], axis=1, keepdims=True))
    stat = jnp.concatenate([stat, jnp.zeros((1, HALF), f32)], axis=1)
    for block in range(3):
        extra_ref[NTP + block : NTP + block + 1] = stat[:, block * COLS : (block + 1) * COLS]
    extra_ref[NTP + 3 :] = gain_own_ref[: EXTRA - NTP - 3]

    grad_w = dot_first(scaled, rows).astype(bf16)
    grad_out = dot_first(mixed_ref[...], grad_attn).astype(bf16)
    for tree in range(NDP):
        trees_ref[tree, :QKV_CHUNK] = grad_w[tree * QKV_CHUNK : (tree + 1) * QKV_CHUNK]
        trees_ref[tree, QKV_CHUNK:] = grad_out[tree * OUT_CHUNK : (tree + 1) * OUT_CHUNK]
    bias = jnp.sum(d_wide, axis=0, keepdims=True)
    bias = jnp.concatenate([bias, jnp.zeros((1, WIDTH - QKV), f32)], axis=1)
    router = dot_plain(router_ref[...], rows_two_ref[...]) * gain_two_ref[...]
    place = lax.broadcasted_iota(jnp.int32, (8, WIDTH), 0)
    router = jnp.where(place == EXPERTS + 1, bias, router)
    tail_ref[...] = router


def first_norm_body(arrived_ref, tokens_ref, inv_ref, grad_res_ref, out_ref, small_ref):
    dn = arrived_ref[0, :ROWS].astype(f32)
    tails = [arrived_ref[chip, ROWS:].astype(f32) for chip in range(NCHIP)]
    for chip in range(1, NCHIP):
        dn = dn + arrived_ref[chip, :ROWS].astype(f32)
    tails = [tail[:EXTRA] + tail[EXTRA:] for tail in tails]
    extra = sum(tails[1:], tails[0])
    stat = jnp.concatenate([extra[NTP + k : NTP + k + 1] for k in range(3)], axis=1)
    stat = to_columns(stat)[:ROWS] * (1.0 / WIDTH)
    inverse = inv_ref[...]
    normed = tokens_ref[...].astype(f32) * inverse
    out_ref[...] = inverse * (dn - normed * stat) + grad_res_ref[...]
    small_ref[...] = jnp.zeros((8, WIDTH), f32)
    for block in range(NTP):
        spot = slice(block * COLS, (block + 1) * COLS)
        small_ref[0:1, spot] = extra[block : block + 1]
        place = NTP + 3 + block % 2
        small_ref[1:2, spot] = tails[block // 2][place : place + 1]


def trees_body(arrived_ref, tail_ref, small_ref, out_ref):
    total = arrived_ref[0].astype(f32)
    for tree in range(1, NDP):
        total = total + arrived_ref[tree].astype(f32)
    low = total.astype(bf16)
    tail = jnp.concatenate([tail_ref[...], small_ref[...]], axis=0).astype(bf16)
    for tree in range(NDP):
        out_ref[tree, : QKV_CHUNK + OUT_CHUNK] = low
        out_ref[tree, QKV_CHUNK + OUT_CHUNK :] = tail


def last_body(
    all_ref, gain_ref, resid_ref, ffn_ref, query_ref, key_ref, value_ref, out_ref, bias_q_ref,
    bias_k_ref, bias_v_ref, router_ref, switch_ref, one_ref, two_ref, output_ref,
):
    mats = jnp.concatenate([all_ref[tree, :QKV_CHUNK] for tree in range(NDP)], axis=0)
    mats = mats.astype(f32) * gain_ref[...]
    query_ref[...] = jnp.transpose(mats[:HDIM])
    key_ref[...] = jnp.transpose(mats[HDIM : 2 * HDIM])
    value_ref[...] = jnp.transpose(mats[2 * HDIM :])
    start = QKV_CHUNK + OUT_CHUNK
    tail = jnp.zeros((16, WIDTH), f32)
    for tree in range(NDP):
        out_ref[tree * OUT_CHUNK : (tree + 1) * OUT_CHUNK] = all_ref[
            tree, QKV_CHUNK:start
        ].astype(f32)
        tail = tail + all_ref[tree, start:].astype(f32)
    router_ref[...] = tail[:EXPERTS]
    switch_ref[...] = tail[EXPERTS : EXPERTS + 1]
    bias = tail[EXPERTS + 1 : EXPERTS + 2]
    bias_q_ref[...] = bias[:, :HDIM]
    bias_k_ref[...] = bias[:, HDIM : 2 * HDIM]
    bias_v_ref[...] = bias[:, 2 * HDIM : QKV]
    one_ref[...] = tail[8:9] / gain_ref[...]
    two_ref[...] = tail[9:10]
    output_ref[...] = (resid_ref[...] + ffn_ref[...].astype(f32)).astype(bf16)


def lay_trees(rows_ref, blocks_ref, trees):
    for tree in range(trees):
        for block in range(NTP):
            rows_ref[tree * ROWS : (tree + 1) * ROWS, block * COLS : (block + 1) * COLS] = (
                blocks_ref[tree, block]
            )


def plain_all_body(blocks_ref, down_ref, out_ref, rows_ref):
    lay_trees(rows_ref, blocks_ref, 2)
    out_ref[...] = dot_last(down_ref[...], rows_ref[...]).astype(bf16)


BLOCK = 512
READY = ((0, 1), (2, 3), (4,), (5, 6), (7,))


def hidden_all_body(
    blocks_ref, plain_ref, chosen_ref, switch_ref, gate_ref, up_ref,
    grad_gate_ref, grad_up_ref, act_ref, rows_ref, sems,
):

    def copies(trees):
        for tree in trees:
            for block in range(NTP):
                where = (
                    slice(tree * ROWS, (tree + 1) * ROWS),
                    slice(block * COLS, (block + 1) * COLS),
                )
                yield pltpu.make_async_copy(
                    blocks_ref.at[tree, block, :ROWS], rows_ref.at[where], sems.at[tree, block]
                )

    step = pl.program_id(0)

    @pl.when(step == 0)
    def _():
        for copy in copies(READY[0]):
            copy.start()

    for number, trees in enumerate(READY):

        @pl.when(step == number)
        def _(number=number, trees=trees):
            for copy in copies(trees):
                copy.wait()
            if number == 0:
                for copy in copies(range(len(READY[0]), NDP)):
                    copy.start()

    spot = pl.ds(pl.multiple_of(step * BLOCK, BLOCK), BLOCK)
    rows = rows_ref[spot, :]
    inverse = to_row(mean_square_inverse(rows))
    _, probs = routing(rows, inverse, switch_ref[...])
    mix = probs * chosen_ref[...]
    half = dot_last(gate_ref[...], rows) * (0.5 * inverse)
    up_val = dot_last(up_ref[...], rows)
    twice = jnp.tanh(half) + 1.0
    silu = half * twice
    weight = per_hidden(mix * inverse)
    act_ref[...] = (weight * (silu * up_val)).astype(bf16)
    grad_act = weight * plain_ref[...].astype(f32)
    grad_up_ref[...] = (grad_act * silu).astype(bf16)
    slope = twice + silu * (2.0 - twice)
    grad_gate_ref[...] = (grad_act * (up_val * (0.5 * inverse)) * slope).astype(bf16)


def weights_body(
    grad_gate_ref, grad_up_ref, act_ref, resid_ref, cot_ref, gain_ref,
    gate_r_ref, gate_s_ref, up_r_ref, up_s_ref, down_r_ref, down_s_ref,
):
    def columns(ref):
        blocks = [ref[:, k].reshape(ALL_ROWS, COLS) for k in range(ref.shape[1])]
        return jnp.concatenate(blocks, axis=1)

    resid = columns(resid_ref)
    gain = gain_ref[...]
    grad = dot_plain(grad_gate_ref[...], resid) * gain
    gate_r_ref[...] = grad[:ROUTED]
    gate_s_ref[...] = grad[ROUTED:]
    grad = dot_plain(grad_up_ref[...], resid) * gain
    up_r_ref[...] = grad[:ROUTED]
    up_s_ref[...] = grad[ROUTED:]
    grad = dot_plain(act_ref[...], columns(cot_ref))
    down_r_ref[...] = grad[:ROUTED]
    down_s_ref[...] = grad[ROUTED:]


def once(shape):
    zero = (0,) * len(shape)
    return pl.BlockSpec(shape, lambda i: zero, pipeline_mode=pl.Buffered(1))


PAIR = 2 * ROWS
PAIR_FLOPS = 2 * HIDDEN * WIDTH * ALL_ROWS


def plain_all(blocks, down_mat):
    return pl.pallas_call(
        plain_all_body,
        grid=(NDP // 2,),
        in_specs=[
            pl.BlockSpec((2, NTP, ROWS, COLS), lambda i: (i, 0, 1, 0)),
            once((HIDDEN, WIDTH)),
        ],
        out_specs=pl.BlockSpec((HIDDEN, PAIR), lambda i: (0, i)),
        out_shape=sds((HIDDEN, ALL_ROWS), bf16),
        scratch_shapes=[pltpu.VMEM((PAIR, WIDTH), bf16)],
        compiler_params=pltpu.CompilerParams(vmem_limit_bytes=60 * MIB),
        cost_estimate=pl.CostEstimate(
            flops=PAIR_FLOPS, bytes_accessed=20 * MIB, transcendentals=0
        ),
    )(blocks, down_mat)


def hidden_all(blocks, plain, chosen, switch_mat, gate_mat, up_mat):
    return pl.pallas_call(
        hidden_all_body,
        grid=(ALL_ROWS // BLOCK,),
        in_specs=[
            pl.BlockSpec(memory_space=pltpu.HBM),
            pl.BlockSpec((HIDDEN, BLOCK), lambda i: (0, i)),
            pl.BlockSpec((8, BLOCK), lambda i: (0, i)),
            once((8, WIDTH)),
            once((HIDDEN, WIDTH)),
            once((HIDDEN, WIDTH)),
        ],
        out_specs=[pl.BlockSpec((HIDDEN, BLOCK), lambda i: (0, i))] * 3,
        out_shape=[sds((HIDDEN, ALL_ROWS), bf16)] * 3,
        scratch_shapes=[
            pltpu.VMEM((ALL_ROWS, WIDTH), bf16),
            pltpu.SemaphoreType.DMA((NDP, NTP)),
        ],
        compiler_params=pltpu.CompilerParams(vmem_limit_bytes=60 * MIB),
        cost_estimate=pl.CostEstimate(
            flops=3 * PAIR_FLOPS, bytes_accessed=40 * MIB, transcendentals=HIDDEN * ALL_ROWS
        ),
    )(blocks, plain, chosen, switch_mat, gate_mat, up_mat)


WIDE = 2


def weight_grads(grad_gate, grad_up, act, blocks, gain):
    step = WIDE * COLS
    resid = pl.BlockSpec((NDP, WIDE, ROWS, COLS), lambda i: (0, i, 0, 0))
    cot = pl.BlockSpec((NDP, WIDE, ROWS, COLS), lambda i: (0, i, 1, 0))
    return pl.pallas_call(
        weights_body,
        grid=(WIDTH // step,),
        in_specs=[
            once((HIDDEN, ALL_ROWS)),
            once((HIDDEN, ALL_ROWS)),
            once((HIDDEN, ALL_ROWS)),
            resid,
            cot,
            pl.BlockSpec((1, step), lambda i: (0, i)),
        ],
        out_specs=[
            pl.BlockSpec((ROUTED, step), lambda i: (0, i)),
            pl.BlockSpec((SHARED, step), lambda i: (0, i)),
        ]
        * 3,
        out_shape=[sds((ROUTED, WIDTH), f32), sds((SHARED, WIDTH), f32)] * 3,
        compiler_params=pltpu.CompilerParams(vmem_limit_bytes=60 * MIB),
        cost_estimate=pl.CostEstimate(
            flops=3 * PAIR_FLOPS, bytes_accessed=56 * MIB, transcendentals=0
        ),
    )(grad_gate, grad_up, act, blocks, blocks, gain)


def widen(block, count):
    return jnp.broadcast_to(block[None], (count,) + block.shape)


def over_chips(blocks):
    return lax.all_to_all(blocks, CHIPS, 0, 0)


def over_trees(blocks):
    return lax.all_to_all(blocks, TREES, 0, 0)


def after(value, *others):
    return lax.optimization_barrier((value,) + others)[0]


def swap(block):
    return lax.ppermute(block, "core", SWAP)


def on_device(
    tokens,
    cotangent,
    routes,
    segments,
    parents,
    positions,
    norm_one,
    w_query,
    b_query,
    w_key,
    b_key,
    w_value,
    b_value,
    w_out,
    norm_two,
    router,
    expert_gate,
    expert_up,
    expert_down,
    shared_gate,
    shared_up,
    shared_down,
    shared_switch,
):
    core = lax.axis_index("core").astype(jnp.int32).reshape(1)
    col_start = lax.axis_index(TENSOR) * COLS
    gain_one = norm_one.astype(f32)
    gain_two = norm_two.astype(f32)

    def to_hidden(routed, shared):
        mat = jnp.concatenate(
            [jnp.transpose(routed, (0, 2, 1)).reshape(ROUTED, WIDTH), shared.T], axis=0
        )
        return (mat.astype(f32) * gain_two).astype(bf16)

    gate_mat = to_hidden(expert_gate, shared_gate)
    up_mat = to_hidden(expert_up, shared_up)
    down_mat = jnp.concatenate([expert_down.reshape(ROUTED, WIDTH), shared_down], axis=0)
    w_qkv = jnp.concatenate([w_query, w_key, w_value], axis=1)
    w_qkv = (w_qkv.astype(f32) * gain_one[:, None]).astype(bf16)
    bias = jnp.concatenate([b_query, b_key, b_value]).astype(f32)[None]
    switch_mat = jnp.concatenate(
        [router.T, shared_switch[None], jnp.zeros((1, WIDTH), bf16)], axis=0
    )
    switch_mat = (switch_mat.astype(f32) * gain_two).astype(bf16)
    switch_cols = lax.dynamic_slice_in_dim(switch_mat, col_start, COLS, 1)
    gain_two_cols = lax.dynamic_slice_in_dim(gain_two, col_start, COLS, 0)[None]
    frequency = jnp.power(THETA, -2.0 * jnp.arange(HALF, dtype=f32) / HDIM)
    angles = positions.astype(f32)[:, None] * frequency[None, :]
    cosine = jnp.cos(angles)
    sine_table = jnp.sin(angles)
    visible = (
        (segments[None, :] == 0)
        | (segments[None, :] == segments[:, None])
        | (segments[None, :] == parents[:, None])
    ) & (positions[None, :] <= positions[:, None])
    visible = visible.astype(f32)
    wide, shown, chosen = call(
        start_body,
        [
            sds((NCHIP, ROWS, COLS), bf16), sds((SHOWN, COLS), bf16), sds((8, ROWS), f32),
        ],
        [tokens, routes.T],
        moved=2 * MIB,
    )
    cot_rows = lax.all_gather(cotangent, TENSOR, axis=1, tiled=True)
    own = over_chips(wide)
    own = after(own, down_mat, w_qkv, bias, cosine, sine_table, visible)
    other = swap(own)
    blocks8 = (NCHIP, ROWS, COLS)
    keep, send, rows_one, inv_one, plain, qkv, probs, mixed = call(
        attend_body,
        [
            sds(blocks8, bf16), sds(blocks8, bf16), sds((ROWS, WIDTH), bf16),
            sds((ROWS, COLS), f32), sds((ROWS, QKV), f32), sds((ROWS, QKV), bf16),
            sds((ROWS, ROWS), f32), sds((ROWS, HDIM), bf16),
        ],
        [core, own, other, w_qkv, bias, cosine, sine_table, visible, w_out],
        smem=1, flops=900_000_000, moved=8 * MIB,
    )
    arrived = over_chips((keep.astype(f32) + swap(send).astype(f32)).astype(bf16))
    grad_plain = call(
        plain_grad_body,
        [sds((HIDDEN, ROWS), bf16)],
        [cot_rows, down_mat],
        flops=2 * HIDDEN * WIDTH * ROWS, moved=6 * MIB,
    )[0]
    resid_cols, wide, tall = call(
        residual_body,
        [sds((ROWS, COLS), f32), sds(blocks8, bf16), sds((TALL, COLS), bf16)],
        [tokens, after(arrived, grad_plain), cotangent, shown],
        moved=2 * MIB,
    )

    own = after(over_chips(wide), gate_mat, up_mat)
    blocks = lax.all_gather(tall, TREES + TENSOR, axis=0).reshape(NDP, NTP, TALL, COLS)
    chosen_all = blocks[:, 0, 2 * ROWS : 2 * ROWS + EXTRA].reshape(NDP, 3, 8, COLS)
    chosen_all = jnp.transpose(chosen_all, (2, 0, 1, 3)).reshape(8, NDP, 3 * COLS)
    chosen_all = chosen_all[:, :, :ROWS].reshape(8, ALL_ROWS).astype(f32)
    (
        keep, send, act, extra, rows_two, inv_two, inv_row, gates, logits,
    ) = call(
        experts_body,
        [
            sds(blocks8, bf16), sds(blocks8, bf16), sds((HIDDEN, ROWS), bf16),
            sds((3, 8, COLS), f32), sds((ROWS, WIDTH), bf16), sds((ROWS, COLS), f32),
            sds((1, ROWS), f32), sds((8, ROWS), f32), sds((8, ROWS), f32),
        ],
        [core, own, swap(own), chosen, switch_mat, gate_mat, up_mat, grad_plain],
        smem=1, flops=8 * HIDDEN * WIDTH * ROWS,
        moved=20 * MIB,
    )
    extra = extra.reshape(EXTRA, COLS)
    payload = call(
        payload_body,
        [sds((NCHIP, SENT, COLS), bf16)],
        [keep, swap(send), extra, swap(extra)],
        moved=4 * MIB, limit=16,
    )[0]
    arrived = over_chips(payload)
    wide, grad_res, router_low, gain_own = call(
        second_norm_body,
        [
            sds(blocks8, bf16), sds((ROWS, COLS), f32), sds((8, ROWS), bf16),
            sds((8, COLS), f32),
        ],
        [
            core, arrived, gates, chosen, logits, inv_row, switch_cols, cotangent,
            resid_cols,
            inv_two, gain_two_cols,
        ],
        smem=1, moved=3 * MIB,
    )
    own = over_chips(wide)
    ffn = call(
        branches_body,
        [sds((NTP * ROWS, COLS), bf16)],
        [after(act, grad_res), down_mat],
        flops=2 * HIDDEN * WIDTH * ROWS, moved=8 * MIB,
    )[0]
    own = after(own, ffn)
    keep, send, extra, trees, tail = pl.pallas_call(
        attend_back_body,
        in_specs=[pl.BlockSpec(memory_space=pltpu.SMEM)]
        + [pl.BlockSpec(memory_space=pltpu.VMEM)] * 16,
        out_specs=[pl.BlockSpec(memory_space=pltpu.VMEM)] * 5,
        out_shape=[
            sds(blocks8, bf16), sds(blocks8, bf16), sds((EXTRA, COLS), f32),
            sds((NDP, QKV_CHUNK + OUT_CHUNK, WIDTH), bf16), sds((8, WIDTH), f32),
        ],
        scratch_shapes=[pltpu.VMEM((ROWS, WIDTH), bf16)],
        compiler_params=pltpu.CompilerParams(vmem_limit_bytes=60 * MIB),
        cost_estimate=pl.CostEstimate(
            flops=2_000_000_000, bytes_accessed=14 * MIB, transcendentals=0
        ),
    )(
        core, own, swap(own), w_out, qkv, probs, plain, inv_one, cosine, sine_table, w_qkv,
        rows_one, gain_own, mixed, router_low, rows_two, gain_two[None],
    )
    payload = call(
        payload_body,
        [sds((NCHIP, SENT, COLS), bf16)],
        [keep, swap(send), extra, swap(extra)],
        moved=4 * MIB, limit=16,
    )[0]
    arrived = over_chips(payload)
    plain_rows = plain_all(after(blocks, payload), down_mat)
    trees = after(trees, plain_rows)
    tree_sums = over_trees(trees)
    grads = hidden_all(
        blocks, after(plain_rows, trees), chosen_all, switch_mat, gate_mat, up_mat
    )
    ffn = lax.psum_scatter(
        after(ffn, blocks, payload), TENSOR, scatter_dimension=0, tiled=True
    )
    input_grad, small = call(
        first_norm_body,
        [sds((ROWS, COLS), f32), sds((8, WIDTH), f32)],
        [after(arrived, plain_rows), tokens, inv_one, grad_res],
        moved=2 * MIB, limit=24,
    )
    chunk = QKV_CHUNK + OUT_CHUNK
    wide = call(
        trees_body,
        [sds((NDP, chunk + 16, WIDTH), bf16)],
        [after(tree_sums, *grads), tail, small],
        moved=6 * MIB, limit=24,
    )[0]
    everything = over_trees(wide)
    (
        grad_query, grad_key, grad_value, grad_out_proj, query_bias, key_bias, value_bias,
        grad_router, grad_switch, gain_one_sum, gain_two_sum, output,
    ) = call(
        last_body,
        [
            sds((WIDTH, HDIM), f32), sds((WIDTH, HDIM), f32), sds((WIDTH, HDIM), f32),
            sds((HDIM, WIDTH), f32), sds((1, HDIM), f32), sds((1, HDIM), f32),
            sds((1, HDIM), f32), sds((EXPERTS, WIDTH), f32), sds((1, WIDTH), f32),
            sds((1, WIDTH), f32), sds((1, WIDTH), f32), sds((ROWS, COLS), bf16),
        ],
        [everything, gain_one[None], resid_cols, ffn],
        moved=7 * MIB, limit=24,
    )

    gate_r, gate_s, up_r, up_s, down_r, down_s = weight_grads(
        after(grads[0], wide, input_grad), *grads[1:], blocks, gain_two[None]
    )

    def routed_cols(mat):
        return jnp.transpose(mat.reshape(EXPERTS, EFF, WIDTH), (0, 2, 1))

    return (
        output,
        input_grad,
        gain_one_sum.reshape(-1),
        grad_query,
        query_bias.reshape(-1),
        grad_key,
        key_bias.reshape(-1),
        grad_value,
        value_bias.reshape(-1),
        grad_out_proj,
        gain_two_sum.reshape(-1),
        grad_router.T,
        routed_cols(gate_r),
        routed_cols(up_r),
        down_r.reshape(EXPERTS, EFF, WIDTH),
        gate_s.T,
        up_s.T,
        down_s,
        grad_switch.reshape(-1),
    )


def solution(mesh):
    fine = Mesh(mesh.devices.reshape(4, 2, 2, 4, 2), TREES + TENSOR)
    both = P(TREES, TENSOR)
    cols = P(None, TENSOR)
    placed = (
        both,
        both,
        P(TREES, None),
        P(TREES),
        P(TREES),
        P(TREES),
        P(),
        cols,
        P(TENSOR),
        cols,
        P(TENSOR),
        cols,
        P(TENSOR),
        P(TENSOR, None),
        P(),
        P(),
        P(None, None, TENSOR),
        P(None, None, TENSOR),
        P(None, TENSOR, None),
        cols,
        cols,
        P(TENSOR, None),
        P(),
    )
    return jax.shard_map(
        on_device,
        mesh=fine,
        in_specs=placed,
        out_specs=(
            both,
            both,
            P(),
            cols,
            P(TENSOR),
            cols,
            P(TENSOR),
            cols,
            P(TENSOR),
            P(TENSOR, None),
            P(),
            P(),
            P(None, None, TENSOR),
            P(None, None, TENSOR),
            P(None, TENSOR, None),
            cols,
            cols,
            P(TENSOR, None),
            P(),
        ),
        check_vma=False,
    )
```

```python
import functools

import jax
import jax.numpy as jnp
from jax import lax
from jax.experimental import pallas as pl
from jax.experimental.pallas import tpu as pltpu
from jax.sharding import Mesh
from jax.sharding import PartitionSpec as P

HDIM = 128
HALF = HDIM // 2
EPSILON = 1e-06
THETA = 1000000.0
NEG_BIG = -1e30
TREES = ("z", "xhi")
CHIPS = ("xlo", "y")
TENSOR = ("xlo", "y", "core")
SWAP = [(0, 1), (1, 0)]
NDP = 8
NCHIP = 8
NTP = 16
ROWS = 320
COLS = 128
WIDTH = 2048
EXPERTS = 6
EFF = 88
ROUTED = EXPERTS * EFF
SHARED = 352
HIDDEN = ROUTED + SHARED
ALL_ROWS = NDP * ROWS
EXTRA = 24
SHOWN = 32
TALL = 2 * ROWS + SHOWN
SENT = ROWS + 2 * EXTRA
QKV = 3 * HDIM
OUT_CHUNK = HDIM // NDP
QKV_CHUNK = QKV // NDP
SCALE = HDIM ** (-0.5)
f32 = jnp.float32
bf16 = jnp.bfloat16
MIB = 1024 * 1024


def dot_plain(left_mat, right_mat):
    return jnp.dot(left_mat, right_mat, preferred_element_type=f32)


def dot_last(left_mat, right_mat):
    return lax.dot_general(
        left_mat, right_mat, (((1,), (1,)), ((), ())), preferred_element_type=f32
    )


def dot_first(left_mat, right_mat):
    return lax.dot_general(
        left_mat, right_mat, (((0,), (0,)), ((), ())), preferred_element_type=f32
    )


def sds(shape, dtype):
    return jax.ShapeDtypeStruct(shape, dtype)


def call(body, out_shape, args, *, smem=0, flops=0, moved=0, limit=60):
    specs = [pl.BlockSpec(memory_space=pltpu.SMEM)] * smem
    specs += [pl.BlockSpec(memory_space=pltpu.VMEM)] * (len(args) - smem)
    return pl.pallas_call(
        body,
        in_specs=specs,
        out_specs=[pl.BlockSpec(memory_space=pltpu.VMEM)] * len(out_shape),
        out_shape=out_shape,
        compiler_params=pltpu.CompilerParams(vmem_limit_bytes=limit * MIB),
        cost_estimate=pl.CostEstimate(flops=flops, bytes_accessed=moved, transcendentals=0),
    )(*args)


def lay_rows(rows_ref, core, own_ref, other_ref, window=slice(0, ROWS)):
    for chip in range(NCHIP):
        own = pl.multiple_of((2 * chip + core) * COLS, COLS)
        other = pl.multiple_of((2 * chip + 1 - core) * COLS, COLS)
        rows_ref[:, pl.ds(own, COLS)] = own_ref[chip, window]
        rows_ref[:, pl.ds(other, COLS)] = other_ref[chip, window]


def part_chips(core, part, keep_ref, send_ref):
    first = core == 0
    for chip in range(NCHIP):
        even = part[:, 2 * chip * COLS : (2 * chip + 1) * COLS]
        odd = part[:, (2 * chip + 1) * COLS : (2 * chip + 2) * COLS]
        keep_ref[chip] = jnp.where(first, even, odd).astype(keep_ref.dtype)
        send_ref[chip] = jnp.where(first, odd, even).astype(send_ref.dtype)


def rotate(rows, cosine, sine_table):
    first, second = rows[:, :HALF], rows[:, HALF:]
    return jnp.concatenate(
        [first * cosine - second * sine_table, second * cosine + first * sine_table], axis=1
    )


def to_row(column):
    return jnp.transpose(jnp.broadcast_to(column, (column.shape[0], COLS)))[:1]


def to_columns(row):
    return jnp.transpose(jnp.broadcast_to(row, (COLS, row.shape[1])))


def sigmoid(values):
    return 0.5 * jnp.tanh(0.5 * values) + 0.5


def per_hidden(weights):
    count = weights.shape[1]
    parts = [jnp.broadcast_to(weights[e : e + 1], (EFF, count)) for e in range(EXPERTS)]
    parts.append(jnp.broadcast_to(weights[EXPERTS : EXPERTS + 1], (SHARED, count)))
    return jnp.concatenate(parts, axis=0)


def routing(rows, inv_row, switch_mat):
    logits = dot_last(switch_mat, rows) * inv_row
    place = lax.broadcasted_iota(jnp.int32, logits.shape, 0)
    shown = jnp.where(place < EXPERTS, logits, NEG_BIG)
    powers = jnp.exp(shown - jnp.max(shown, axis=0, keepdims=True))
    probs = powers / jnp.sum(powers, axis=0, keepdims=True)
    return logits, jnp.where(place == EXPERTS, sigmoid(logits), probs)


def mean_square_inverse(rows):
    wide = rows.astype(f32)
    return lax.rsqrt(jnp.sum(wide * wide, axis=1, keepdims=True) * (1.0 / WIDTH) + EPSILON)


def attend_body(
    core_ref, own_ref, other_ref, w_ref, bias_ref, cos_ref, sin_ref, see_ref, w_out_ref,
    keep_ref, send_ref, rows_ref, inv_ref, plain_ref, qkv_ref, probs_ref, mixed_ref,
):
    core = core_ref[0]
    lay_rows(rows_ref, core, own_ref, other_ref)
    rows = rows_ref[...]
    inverse = mean_square_inverse(rows)
    inv_ref[...] = jnp.broadcast_to(inverse, (ROWS, COLS))
    plain = dot_plain(rows, w_ref[...]) * inverse
    plain_ref[...] = plain
    biased = plain + bias_ref[...]
    cosine, sine_table = cos_ref[...], sin_ref[...]
    query = rotate(biased[:, :HDIM], cosine, sine_table).astype(bf16)
    keys = rotate(biased[:, HDIM : 2 * HDIM], cosine, sine_table).astype(bf16)
    values = biased[:, 2 * HDIM :].astype(bf16)
    qkv_ref[:, :HDIM] = query
    qkv_ref[:, HDIM : 2 * HDIM] = keys
    qkv_ref[:, 2 * HDIM :] = values
    scores = dot_last(query, keys) * SCALE
    masked = jnp.where(see_ref[...] > 0.5, scores, NEG_BIG)
    powers = jnp.exp(masked - jnp.max(masked, axis=1, keepdims=True))
    probs = powers / jnp.sum(powers, axis=1, keepdims=True)
    probs_ref[...] = probs
    mixed = dot_plain(probs.astype(bf16), values).astype(bf16)
    mixed_ref[...] = mixed
    part_chips(core, dot_plain(mixed, w_out_ref[...]), keep_ref, send_ref)


def start_body(tokens_ref, routes_ref, wide_ref, shown_ref, chosen_ref):
    tokens = tokens_ref[...]
    place = lax.broadcasted_iota(jnp.int32, (8, ROWS), 0)
    routes = routes_ref[...]
    found = place >= EXPERTS
    for choice in range(routes.shape[0]):
        found = found | (place == routes[choice : choice + 1])
    chosen = jnp.where(found, 1.0, 0.0)
    chosen_ref[...] = chosen
    last = jnp.concatenate([chosen[:, 2 * COLS :], jnp.zeros((8, HALF), f32)], axis=1)
    shown = [chosen[:, :COLS], chosen[:, COLS : 2 * COLS], last, jnp.zeros((8, COLS), f32)]
    shown_ref[...] = jnp.concatenate(shown, axis=0).astype(bf16)
    for chip in range(NCHIP):
        wide_ref[chip] = tokens


def residual_body(
    tokens_ref, arrived_ref, cot_ref, shown_ref, resid_ref, wide_ref, tall_ref
):
    total = tokens_ref[...].astype(f32)
    for chip in range(NCHIP):
        total = total + arrived_ref[chip].astype(f32)
    resid_ref[...] = total
    low = total.astype(bf16)
    tall_ref[:ROWS] = low
    tall_ref[ROWS : 2 * ROWS] = cot_ref[...]
    tall_ref[2 * ROWS :] = shown_ref[...]
    for chip in range(NCHIP):
        wide_ref[chip] = low


def plain_grad_body(rows_ref, down_ref, out_ref):
    out_ref[...] = dot_last(down_ref[...], rows_ref[...]).astype(bf16)


def experts_body(
    core_ref, own_ref, other_ref, chosen_ref, switch_ref, gate_ref, up_ref, plain_ref,
    keep_ref, send_ref, act_ref, extra_ref, rows_ref, inv_ref, inv_row_ref, probs_ref, logits_ref,
):
    core = core_ref[0]
    lay_rows(rows_ref, core, own_ref, other_ref)
    rows = rows_ref[...]
    inverse = mean_square_inverse(rows)
    inv_ref[...] = jnp.broadcast_to(inverse, (ROWS, COLS))
    inv_row = to_row(inverse)
    inv_row_ref[...] = inv_row
    logits, probs = routing(rows, inv_row, switch_ref[...])
    logits_ref[...] = logits
    probs_ref[...] = probs
    mixing = probs * chosen_ref[...]
    gate_val = dot_last(gate_ref[...], rows) * inv_row
    up_val = dot_last(up_ref[...], rows) * inv_row
    spread_mix = per_hidden(mixing)
    sigma = sigmoid(gate_val)
    silu = gate_val * sigma
    act = silu * up_val
    grad_plain = plain_ref[...].astype(f32)
    pair = act * grad_plain
    grad_act = spread_mix * grad_plain
    grad_gate = grad_act * up_val * (sigma + silu * (1.0 - sigma))
    grad_up = grad_act * silu
    sums = [
        jnp.sum(pair[e * EFF : (e + 1) * EFF], axis=0, keepdims=True) for e in range(EXPERTS)
    ]
    sums.append(jnp.sum(pair[ROUTED:], axis=0, keepdims=True))
    sums.append(jnp.sum(grad_gate * gate_val + grad_up * up_val, axis=0, keepdims=True))
    sums = jnp.concatenate(sums, axis=0)
    extra_ref[0] = sums[:, :COLS]
    extra_ref[1] = sums[:, COLS : 2 * COLS]
    extra_ref[2] = jnp.concatenate([sums[:, 2 * COLS :], jnp.zeros((8, HALF), f32)], axis=1)
    act_ref[...] = (spread_mix * act).astype(bf16)
    part = dot_first(grad_gate.astype(bf16), gate_ref[...])
    part = part + dot_first(grad_up.astype(bf16), up_ref[...])
    part_chips(core, part, keep_ref, send_ref)


def branches_body(act_ref, down_ref, out_ref):
    part = dot_first(act_ref[...], down_ref[...]).astype(bf16)
    for block in range(NTP):
        out_ref[block * ROWS : (block + 1) * ROWS] = part[:, block * COLS : (block + 1) * COLS]


def payload_body(keep_ref, came_ref, extra_ref, extra_came_ref, out_ref):
    extra = extra_ref[...] + extra_came_ref[...]
    high = extra.astype(bf16)
    low = (extra - high.astype(f32)).astype(bf16)
    for chip in range(NCHIP):
        out_ref[chip, :ROWS] = (
            keep_ref[chip].astype(f32) + came_ref[chip].astype(f32)
        ).astype(bf16)
        out_ref[chip, ROWS:] = jnp.concatenate([high, low], axis=0)


def second_norm_body(
    core_ref, arrived_ref, probs_ref, chosen_ref, logits_ref, inv_row_ref, switch_ref, cot_ref,
    resid_ref, inv_ref, gain_ref, wide_ref, grad_ref, router_ref, extra_ref,
):
    dn = arrived_ref[0, :ROWS].astype(f32)
    extra = arrived_ref[0, ROWS:].astype(f32)
    for chip in range(1, NCHIP):
        dn = dn + arrived_ref[chip, :ROWS].astype(f32)
        extra = extra + arrived_ref[chip, ROWS:].astype(f32)
    extra = extra[:EXTRA] + extra[EXTRA:]
    sums = jnp.concatenate([extra[:8], extra[8:16], extra[16:24]], axis=1)[:, :ROWS]
    place = lax.broadcasted_iota(jnp.int32, (8, ROWS), 0)
    probs = probs_ref[...]
    routed = place < EXPERTS
    weighed = jnp.where(routed, probs * (sums * chosen_ref[...]), 0.0)
    total = jnp.sum(weighed, axis=0, keepdims=True)
    low = jnp.where(routed, weighed - probs * total, sums * probs * (1.0 - probs))
    low = jnp.where(place <= EXPERTS, low, 0.0).astype(bf16)
    low_wide = low.astype(f32)
    router_ref[...] = (low_wide * inv_row_ref[...]).astype(bf16)
    dn = dn + dot_first(low, switch_ref[...])
    stat = sums[EXPERTS + 1 :] + jnp.sum(low_wide * logits_ref[...], axis=0, keepdims=True)
    inverse = inv_ref[...]
    normed = resid_ref[...].astype(bf16).astype(f32) * inverse
    own = jnp.sum(dn * normed, axis=0, keepdims=True) / gain_ref[...]
    first = core_ref[0] == 0
    spot = lax.broadcasted_iota(jnp.int32, (8, COLS), 0)
    extra_ref[...] = jnp.where(spot == jnp.where(first, 0, 1), own, 0.0)
    grad = inverse * (dn - normed * (to_columns(stat) * (1.0 / WIDTH)))
    grad = grad + cot_ref[...].astype(f32)
    grad_ref[...] = grad
    low_grad = grad.astype(bf16)
    for chip in range(NCHIP):
        wide_ref[chip] = low_grad


def attend_back_body(
    core_ref, own_ref, other_ref, w_out_ref, qkv_ref, probs_ref, plain_ref, inv_ref, cos_ref,
    sin_ref, w_ref, rows_ref, gain_own_ref, mixed_ref, router_ref, rows_two_ref, gain_two_ref,
    keep_ref, send_ref, extra_ref, trees_ref, tail_ref, grad_rows_ref,
):
    core = core_ref[0]
    lay_rows(grad_rows_ref, core, own_ref, other_ref)
    grad_attn = grad_rows_ref[...]
    query, keys = qkv_ref[:, :HDIM], qkv_ref[:, HDIM : 2 * HDIM]
    values = qkv_ref[:, 2 * HDIM :]
    probs = probs_ref[...]
    heads = dot_last(grad_attn, w_out_ref[...]).astype(bf16)
    dprobs = dot_last(heads, values)
    dscores = probs * (dprobs - jnp.sum(probs * dprobs, axis=1, keepdims=True))
    dscores = dscores.astype(bf16)
    cosine, sine_table = cos_ref[...], -sin_ref[...]
    dq = rotate(dot_plain(dscores, keys) * SCALE, cosine, sine_table)
    dk = rotate(dot_first(dscores, query) * SCALE, cosine, sine_table)
    dv = dot_first(probs.astype(bf16), heads)
    d_low = jnp.concatenate([dq, dk, dv], axis=1).astype(bf16)
    d_wide = d_low.astype(f32)
    inverse = inv_ref[...]
    scaled = (d_wide * jnp.concatenate([inverse] * 3, axis=1)).astype(bf16)
    part = dot_last(d_low, w_ref[...])
    part_chips(core, part, keep_ref, send_ref)
    rows = rows_ref[...]
    normed = rows.astype(f32) * inverse[:, :1]
    gains = jnp.sum(part * normed, axis=0, keepdims=True)
    for block in range(NTP):
        extra_ref[block : block + 1] = gains[:, block * COLS : (block + 1) * COLS]
    stat = to_row(jnp.sum(d_wide * plain_ref[...], axis=1, keepdims=True))
    stat = jnp.concatenate([stat, jnp.zeros((1, HALF), f32)], axis=1)
    for block in range(3):
        extra_ref[NTP + block : NTP + block + 1] = stat[:, block * COLS : (block + 1) * COLS]
    extra_ref[NTP + 3 :] = gain_own_ref[: EXTRA - NTP - 3]

    grad_w = dot_first(scaled, rows).astype(bf16)
    grad_out = dot_first(mixed_ref[...], grad_attn).astype(bf16)
    for tree in range(NDP):
        trees_ref[tree, :QKV_CHUNK] = grad_w[tree * QKV_CHUNK : (tree + 1) * QKV_CHUNK]
        trees_ref[tree, QKV_CHUNK:] = grad_out[tree * OUT_CHUNK : (tree + 1) * OUT_CHUNK]
    bias = jnp.sum(d_wide, axis=0, keepdims=True)
    bias = jnp.concatenate([bias, jnp.zeros((1, WIDTH - QKV), f32)], axis=1)
    router = dot_plain(router_ref[...], rows_two_ref[...]) * gain_two_ref[...]
    place = lax.broadcasted_iota(jnp.int32, (8, WIDTH), 0)
    router = jnp.where(place == EXPERTS + 1, bias, router)
    tail_ref[...] = router


def first_norm_body(arrived_ref, tokens_ref, inv_ref, grad_res_ref, out_ref, small_ref):
    dn = arrived_ref[0, :ROWS].astype(f32)
    tails = [arrived_ref[chip, ROWS:].astype(f32) for chip in range(NCHIP)]
    for chip in range(1, NCHIP):
        dn = dn + arrived_ref[chip, :ROWS].astype(f32)
    tails = [tail[:EXTRA] + tail[EXTRA:] for tail in tails]
    extra = sum(tails[1:], tails[0])
    stat = jnp.concatenate([extra[NTP + k : NTP + k + 1] for k in range(3)], axis=1)
    stat = to_columns(stat)[:ROWS] * (1.0 / WIDTH)
    inverse = inv_ref[...]
    normed = tokens_ref[...].astype(f32) * inverse
    out_ref[...] = inverse * (dn - normed * stat) + grad_res_ref[...]
    small_ref[...] = jnp.zeros((8, WIDTH), f32)
    for block in range(NTP):
        spot = slice(block * COLS, (block + 1) * COLS)
        small_ref[0:1, spot] = extra[block : block + 1]
        place = NTP + 3 + block % 2
        small_ref[1:2, spot] = tails[block // 2][place : place + 1]


def trees_body(arrived_ref, tail_ref, small_ref, out_ref):
    total = arrived_ref[0].astype(f32)
    for tree in range(1, NDP):
        total = total + arrived_ref[tree].astype(f32)
    low = total.astype(bf16)
    tail = jnp.concatenate([tail_ref[...], small_ref[...]], axis=0).astype(bf16)
    for tree in range(NDP):
        out_ref[tree, : QKV_CHUNK + OUT_CHUNK] = low
        out_ref[tree, QKV_CHUNK + OUT_CHUNK :] = tail


def last_body(
    all_ref, gain_ref, resid_ref, ffn_ref, query_ref, key_ref, value_ref, out_ref, bias_q_ref,
    bias_k_ref, bias_v_ref, router_ref, switch_ref, one_ref, two_ref, output_ref,
):
    mats = jnp.concatenate([all_ref[tree, :QKV_CHUNK] for tree in range(NDP)], axis=0)
    mats = mats.astype(f32) * gain_ref[...]
    query_ref[...] = jnp.transpose(mats[:HDIM])
    key_ref[...] = jnp.transpose(mats[HDIM : 2 * HDIM])
    value_ref[...] = jnp.transpose(mats[2 * HDIM :])
    start = QKV_CHUNK + OUT_CHUNK
    tail = jnp.zeros((16, WIDTH), f32)
    for tree in range(NDP):
        out_ref[tree * OUT_CHUNK : (tree + 1) * OUT_CHUNK] = all_ref[
            tree, QKV_CHUNK:start
        ].astype(f32)
        tail = tail + all_ref[tree, start:].astype(f32)
    router_ref[...] = tail[:EXPERTS]
    switch_ref[...] = tail[EXPERTS : EXPERTS + 1]
    bias = tail[EXPERTS + 1 : EXPERTS + 2]
    bias_q_ref[...] = bias[:, :HDIM]
    bias_k_ref[...] = bias[:, HDIM : 2 * HDIM]
    bias_v_ref[...] = bias[:, 2 * HDIM : QKV]
    one_ref[...] = tail[8:9] / gain_ref[...]
    two_ref[...] = tail[9:10]
    output_ref[...] = (resid_ref[...] + ffn_ref[...].astype(f32)).astype(bf16)


def lay_trees(rows_ref, blocks_ref, trees):
    for tree in range(trees):
        for block in range(NTP):
            rows_ref[tree * ROWS : (tree + 1) * ROWS, block * COLS : (block + 1) * COLS] = (
                blocks_ref[tree, block]
            )


def plain_all_body(blocks_ref, shown_ref, down_ref, out_ref, chosen_ref, rows_ref):
    lay_trees(rows_ref, blocks_ref, GROUP)
    chosen = []
    for tree in range(GROUP):
        shown = shown_ref[tree, 0].astype(f32)
        chosen.append(
            jnp.concatenate([shown[:8], shown[8:16], shown[16:24]], axis=1)[:, :ROWS]
        )
    chosen_ref[...] = jnp.concatenate(chosen, axis=1)
    out_ref[...] = dot_last(down_ref[...], rows_ref[...]).astype(bf16)


BLOCK = 512
READY = ((0, 1), (2, 3), (4,), (5, 6), (7,))


def hidden_all_body(
    blocks_ref, plain_ref, chosen_ref, switch_ref, gate_ref, up_ref,
    grad_gate_ref, grad_up_ref, act_ref, rows_ref, sems,
):

    def copies(trees):
        for tree in trees:
            for block in range(NTP):
                where = (
                    slice(tree * ROWS, (tree + 1) * ROWS),
                    slice(block * COLS, (block + 1) * COLS),
                )
                yield pltpu.make_async_copy(
                    blocks_ref.at[tree, block, :ROWS], rows_ref.at[where], sems.at[tree, block]
                )

    step = pl.program_id(0)

    @pl.when(step == 0)
    def _():
        for copy in copies(READY[0]):
            copy.start()

    for number, trees in enumerate(READY):

        @pl.when(step == number)
        def _(number=number, trees=trees):
            for copy in copies(trees):
                copy.wait()
            if number == 0:
                for copy in copies(range(len(READY[0]), NDP)):
                    copy.start()

    spot = pl.ds(pl.multiple_of(step * BLOCK, BLOCK), BLOCK)
    rows = rows_ref[spot, :]
    inverse = to_row(mean_square_inverse(rows))
    _, probs = routing(rows, inverse, switch_ref[...])
    mix = probs * chosen_ref[...]
    half = dot_last(gate_ref[...], rows) * (0.5 * inverse)
    up_val = dot_last(up_ref[...], rows)
    twice = jnp.tanh(half) + 1.0
    silu = half * twice
    weight = per_hidden(mix * inverse)
    act_ref[...] = (weight * (silu * up_val)).astype(bf16)
    grad_act = weight * plain_ref[...].astype(f32)
    grad_up_ref[...] = (grad_act * silu).astype(bf16)
    slope = twice + silu * (2.0 - twice)
    grad_gate_ref[...] = (grad_act * (up_val * (0.5 * inverse)) * slope).astype(bf16)


def weights_body(
    grad_gate_ref, grad_up_ref, act_ref, resid_ref, cot_ref, gain_ref,
    gate_r_ref, gate_s_ref, up_r_ref, up_s_ref, down_r_ref, down_s_ref,
):
    def columns(ref):
        blocks = [ref[:, k].reshape(ALL_ROWS, COLS) for k in range(ref.shape[1])]
        return jnp.concatenate(blocks, axis=1)

    resid = columns(resid_ref)
    gain = gain_ref[...]
    grad = dot_plain(grad_gate_ref[...], resid) * gain
    gate_r_ref[...] = grad[:ROUTED]
    gate_s_ref[...] = grad[ROUTED:]
    grad = dot_plain(grad_up_ref[...], resid) * gain
    up_r_ref[...] = grad[:ROUTED]
    up_s_ref[...] = grad[ROUTED:]
    grad = dot_plain(act_ref[...], columns(cot_ref))
    down_r_ref[...] = grad[:ROUTED]
    down_s_ref[...] = grad[ROUTED:]


def once(shape):
    zero = (0,) * len(shape)
    return pl.BlockSpec(shape, lambda i: zero, pipeline_mode=pl.Buffered(1))


GROUP = 4
TOGETHER = GROUP * ROWS
PAIR_FLOPS = 2 * HIDDEN * WIDTH * ALL_ROWS


def plain_all(blocks, down_mat):
    return pl.pallas_call(
        plain_all_body,
        grid=(NDP // GROUP,),
        in_specs=[
            pl.BlockSpec((GROUP, NTP, ROWS, COLS), lambda i: (i, 0, 1, 0)),
            pl.BlockSpec((GROUP, 1, SHOWN, COLS), lambda i: (i, 0, 2 * ROWS // SHOWN, 0)),
            once((HIDDEN, WIDTH)),
        ],
        out_specs=[
            pl.BlockSpec((HIDDEN, TOGETHER), lambda i: (0, i)),
            pl.BlockSpec((8, TOGETHER), lambda i: (0, i)),
        ],
        out_shape=[sds((HIDDEN, ALL_ROWS), bf16), sds((8, ALL_ROWS), f32)],
        scratch_shapes=[pltpu.VMEM((TOGETHER, WIDTH), bf16)],
        compiler_params=pltpu.CompilerParams(vmem_limit_bytes=60 * MIB),
        cost_estimate=pl.CostEstimate(
            flops=PAIR_FLOPS, bytes_accessed=20 * MIB, transcendentals=0
        ),
    )(blocks, blocks, down_mat)


def hidden_all(blocks, plain, chosen, switch_mat, gate_mat, up_mat):
    return pl.pallas_call(
        hidden_all_body,
        grid=(ALL_ROWS // BLOCK,),
        in_specs=[
            pl.BlockSpec(memory_space=pltpu.HBM),
            pl.BlockSpec((HIDDEN, BLOCK), lambda i: (0, i)),
            pl.BlockSpec((8, BLOCK), lambda i: (0, i)),
            once((8, WIDTH)),
            once((HIDDEN, WIDTH)),
            once((HIDDEN, WIDTH)),
        ],
        out_specs=[pl.BlockSpec((HIDDEN, BLOCK), lambda i: (0, i))] * 3,
        out_shape=[sds((HIDDEN, ALL_ROWS), bf16)] * 3,
        scratch_shapes=[
            pltpu.VMEM((ALL_ROWS, WIDTH), bf16),
            pltpu.SemaphoreType.DMA((NDP, NTP)),
        ],
        compiler_params=pltpu.CompilerParams(vmem_limit_bytes=60 * MIB),
        cost_estimate=pl.CostEstimate(
            flops=3 * PAIR_FLOPS, bytes_accessed=40 * MIB, transcendentals=HIDDEN * ALL_ROWS
        ),
    )(blocks, plain, chosen, switch_mat, gate_mat, up_mat)


WIDE = 2


def weight_grads(grad_gate, grad_up, act, blocks, gain):
    step = WIDE * COLS
    resid = pl.BlockSpec((NDP, WIDE, ROWS, COLS), lambda i: (0, i, 0, 0))
    cot = pl.BlockSpec((NDP, WIDE, ROWS, COLS), lambda i: (0, i, 1, 0))
    return pl.pallas_call(
        weights_body,
        grid=(WIDTH // step,),
        in_specs=[
            once((HIDDEN, ALL_ROWS)),
            once((HIDDEN, ALL_ROWS)),
            once((HIDDEN, ALL_ROWS)),
            resid,
            cot,
            pl.BlockSpec((1, step), lambda i: (0, i)),
        ],
        out_specs=[
            pl.BlockSpec((ROUTED, step), lambda i: (0, i)),
            pl.BlockSpec((SHARED, step), lambda i: (0, i)),
        ]
        * 3,
        out_shape=[sds((ROUTED, WIDTH), f32), sds((SHARED, WIDTH), f32)] * 3,
        compiler_params=pltpu.CompilerParams(vmem_limit_bytes=60 * MIB),
        cost_estimate=pl.CostEstimate(
            flops=3 * PAIR_FLOPS, bytes_accessed=56 * MIB, transcendentals=0
        ),
    )(grad_gate, grad_up, act, blocks, blocks, gain)


def widen(block, count):
    return jnp.broadcast_to(block[None], (count,) + block.shape)


def over_chips(blocks):
    return lax.all_to_all(blocks, CHIPS, 0, 0)


def over_trees(blocks):
    return lax.all_to_all(blocks, TREES, 0, 0)


def after(value, *others):
    return lax.optimization_barrier((value,) + others)[0]


def swap(block):
    return lax.ppermute(block, "core", SWAP)


def on_device(
    tokens,
    cotangent,
    routes,
    segments,
    parents,
    positions,
    norm_one,
    w_query,
    b_query,
    w_key,
    b_key,
    w_value,
    b_value,
    w_out,
    norm_two,
    router,
    expert_gate,
    expert_up,
    expert_down,
    shared_gate,
    shared_up,
    shared_down,
    shared_switch,
):
    core = lax.axis_index("core").astype(jnp.int32).reshape(1)
    col_start = lax.axis_index(TENSOR) * COLS
    gain_one = norm_one.astype(f32)
    gain_two = norm_two.astype(f32)

    def to_hidden(routed, shared):
        mat = jnp.concatenate(
            [jnp.transpose(routed, (0, 2, 1)).reshape(ROUTED, WIDTH), shared.T], axis=0
        )
        return (mat.astype(f32) * gain_two).astype(bf16)

    gate_mat = to_hidden(expert_gate, shared_gate)
    up_mat = to_hidden(expert_up, shared_up)
    down_mat = jnp.concatenate([expert_down.reshape(ROUTED, WIDTH), shared_down], axis=0)
    w_qkv = jnp.concatenate([w_query, w_key, w_value], axis=1)
    w_qkv = (w_qkv.astype(f32) * gain_one[:, None]).astype(bf16)
    bias = jnp.concatenate([b_query, b_key, b_value]).astype(f32)[None]
    switch_mat = jnp.concatenate(
        [router.T, shared_switch[None], jnp.zeros((1, WIDTH), bf16)], axis=0
    )
    switch_mat = (switch_mat.astype(f32) * gain_two).astype(bf16)
    switch_cols = lax.dynamic_slice_in_dim(switch_mat, col_start, COLS, 1)
    gain_two_cols = lax.dynamic_slice_in_dim(gain_two, col_start, COLS, 0)[None]
    frequency = jnp.power(THETA, -2.0 * jnp.arange(HALF, dtype=f32) / HDIM)
    angles = positions.astype(f32)[:, None] * frequency[None, :]
    cosine = jnp.cos(angles)
    sine_table = jnp.sin(angles)
    visible = (
        (segments[None, :] == 0)
        | (segments[None, :] == segments[:, None])
        | (segments[None, :] == parents[:, None])
    ) & (positions[None, :] <= positions[:, None])
    visible = visible.astype(f32)
    wide, shown, chosen = call(
        start_body,
        [
            sds((NCHIP, ROWS, COLS), bf16), sds((SHOWN, COLS), bf16), sds((8, ROWS), f32),
        ],
        [tokens, routes.T],
        moved=2 * MIB,
    )
    cot_rows = lax.all_gather(cotangent, TENSOR, axis=1, tiled=True)
    own = over_chips(wide)
    own = after(own, down_mat, w_qkv, bias, cosine, sine_table, visible)
    other = swap(own)
    blocks8 = (NCHIP, ROWS, COLS)
    keep, send, rows_one, inv_one, plain, qkv, probs, mixed = call(
        attend_body,
        [
            sds(blocks8, bf16), sds(blocks8, bf16), sds((ROWS, WIDTH), bf16),
            sds((ROWS, COLS), f32), sds((ROWS, QKV), f32), sds((ROWS, QKV), bf16),
            sds((ROWS, ROWS), f32), sds((ROWS, HDIM), bf16),
        ],
        [core, own, other, w_qkv, bias, cosine, sine_table, visible, w_out],
        smem=1, flops=900_000_000, moved=8 * MIB,
    )
    arrived = over_chips((keep.astype(f32) + swap(send).astype(f32)).astype(bf16))
    grad_plain = call(
        plain_grad_body,
        [sds((HIDDEN, ROWS), bf16)],
        [cot_rows, down_mat],
        flops=2 * HIDDEN * WIDTH * ROWS, moved=6 * MIB,
    )[0]
    resid_cols, wide, tall = call(
        residual_body,
        [sds((ROWS, COLS), f32), sds(blocks8, bf16), sds((TALL, COLS), bf16)],
        [tokens, after(arrived, grad_plain), cotangent, shown],
        moved=2 * MIB,
    )

    own = after(over_chips(wide), gate_mat, up_mat)
    blocks = lax.all_gather(tall, TREES + TENSOR, axis=0).reshape(NDP, NTP, TALL, COLS)
    (
        keep, send, act, extra, rows_two, inv_two, inv_row, gates, logits,
    ) = call(
        experts_body,
        [
            sds(blocks8, bf16), sds(blocks8, bf16), sds((HIDDEN, ROWS), bf16),
            sds((3, 8, COLS), f32), sds((ROWS, WIDTH), bf16), sds((ROWS, COLS), f32),
            sds((1, ROWS), f32), sds((8, ROWS), f32), sds((8, ROWS), f32),
        ],
        [core, own, swap(own), chosen, switch_mat, gate_mat, up_mat, grad_plain],
        smem=1, flops=8 * HIDDEN * WIDTH * ROWS,
        moved=20 * MIB,
    )
    extra = extra.reshape(EXTRA, COLS)
    payload = call(
        payload_body,
        [sds((NCHIP, SENT, COLS), bf16)],
        [keep, swap(send), extra, swap(extra)],
        moved=4 * MIB, limit=16,
    )[0]
    arrived = over_chips(payload)
    wide, grad_res, router_low, gain_own = call(
        second_norm_body,
        [
            sds(blocks8, bf16), sds((ROWS, COLS), f32), sds((8, ROWS), bf16),
            sds((8, COLS), f32),
        ],
        [
            core, arrived, gates, chosen, logits, inv_row, switch_cols, cotangent,
            resid_cols,
            inv_two, gain_two_cols,
        ],
        smem=1, moved=3 * MIB,
    )
    own = over_chips(wide)
    ffn = call(
        branches_body,
        [sds((NTP * ROWS, COLS), bf16)],
        [after(act, grad_res), down_mat],
        flops=2 * HIDDEN * WIDTH * ROWS, moved=8 * MIB,
    )[0]
    own = after(own, ffn)
    keep, send, extra, trees, tail = pl.pallas_call(
        attend_back_body,
        in_specs=[pl.BlockSpec(memory_space=pltpu.SMEM)]
        + [pl.BlockSpec(memory_space=pltpu.VMEM)] * 16,
        out_specs=[pl.BlockSpec(memory_space=pltpu.VMEM)] * 5,
        out_shape=[
            sds(blocks8, bf16), sds(blocks8, bf16), sds((EXTRA, COLS), f32),
            sds((NDP, QKV_CHUNK + OUT_CHUNK, WIDTH), bf16), sds((8, WIDTH), f32),
        ],
        scratch_shapes=[pltpu.VMEM((ROWS, WIDTH), bf16)],
        compiler_params=pltpu.CompilerParams(vmem_limit_bytes=60 * MIB),
        cost_estimate=pl.CostEstimate(
            flops=2_000_000_000, bytes_accessed=14 * MIB, transcendentals=0
        ),
    )(
        core, own, swap(own), w_out, qkv, probs, plain, inv_one, cosine, sine_table, w_qkv,
        rows_one, gain_own, mixed, router_low, rows_two, gain_two[None],
    )
    payload = call(
        payload_body,
        [sds((NCHIP, SENT, COLS), bf16)],
        [keep, swap(send), extra, swap(extra)],
        moved=4 * MIB, limit=16,
    )[0]
    arrived = over_chips(payload)
    plain_rows, chosen_all = plain_all(after(blocks, payload), down_mat)
    trees = after(trees, plain_rows)
    tree_sums = over_trees(trees)
    grads = hidden_all(
        blocks, after(plain_rows, trees), chosen_all, switch_mat, gate_mat, up_mat
    )
    ffn = lax.psum_scatter(
        after(ffn, blocks, payload), TENSOR, scatter_dimension=0, tiled=True
    )
    input_grad, small = call(
        first_norm_body,
        [sds((ROWS, COLS), f32), sds((8, WIDTH), f32)],
        [after(arrived, plain_rows), tokens, inv_one, grad_res],
        moved=2 * MIB, limit=24,
    )
    chunk = QKV_CHUNK + OUT_CHUNK
    wide = call(
        trees_body,
        [sds((NDP, chunk + 16, WIDTH), bf16)],
        [after(tree_sums, *grads), tail, small],
        moved=6 * MIB, limit=24,
    )[0]
    everything = over_trees(wide)
    (
        grad_query, grad_key, grad_value, grad_out_proj, query_bias, key_bias, value_bias,
        grad_router, grad_switch, gain_one_sum, gain_two_sum, output,
    ) = call(
        last_body,
        [
            sds((WIDTH, HDIM), f32), sds((WIDTH, HDIM), f32), sds((WIDTH, HDIM), f32),
            sds((HDIM, WIDTH), f32), sds((1, HDIM), f32), sds((1, HDIM), f32),
            sds((1, HDIM), f32), sds((EXPERTS, WIDTH), f32), sds((1, WIDTH), f32),
            sds((1, WIDTH), f32), sds((1, WIDTH), f32), sds((ROWS, COLS), bf16),
        ],
        [everything, gain_one[None], resid_cols, ffn],
        moved=7 * MIB, limit=24,
    )

    gate_r, gate_s, up_r, up_s, down_r, down_s = weight_grads(
        after(grads[0], wide, input_grad), *grads[1:], blocks, gain_two[None]
    )

    def routed_cols(mat):
        return jnp.transpose(mat.reshape(EXPERTS, EFF, WIDTH), (0, 2, 1))

    return (
        output,
        input_grad,
        gain_one_sum.reshape(-1),
        grad_query,
        query_bias.reshape(-1),
        grad_key,
        key_bias.reshape(-1),
        grad_value,
        value_bias.reshape(-1),
        grad_out_proj,
        gain_two_sum.reshape(-1),
        grad_router.T,
        routed_cols(gate_r),
        routed_cols(up_r),
        down_r.reshape(EXPERTS, EFF, WIDTH),
        gate_s.T,
        up_s.T,
        down_s,
        grad_switch.reshape(-1),
    )


def solution(mesh):
    fine = Mesh(mesh.devices.reshape(4, 2, 2, 4, 2), TREES + TENSOR)
    both = P(TREES, TENSOR)
    cols = P(None, TENSOR)
    placed = (
        both,
        both,
        P(TREES, None),
        P(TREES),
        P(TREES),
        P(TREES),
        P(),
        cols,
        P(TENSOR),
        cols,
        P(TENSOR),
        cols,
        P(TENSOR),
        P(TENSOR, None),
        P(),
        P(),
        P(None, None, TENSOR),
        P(None, None, TENSOR),
        P(None, TENSOR, None),
        cols,
        cols,
        P(TENSOR, None),
        P(),
    )
    return jax.shard_map(
        on_device,
        mesh=fine,
        in_specs=placed,
        out_specs=(
            both,
            both,
            P(),
            cols,
            P(TENSOR),
            cols,
            P(TENSOR),
            cols,
            P(TENSOR),
            P(TENSOR, None),
            P(),
            P(),
            P(None, None, TENSOR),
            P(None, None, TENSOR),
            P(None, TENSOR, None),
            cols,
            cols,
            P(TENSOR, None),
            P(),
        ),
        check_vma=False,
    )
```
